128 devices in a mesh: stn: 32 (over y_hi, x, z), tm: 4 (over y_lo, core).
Axes of the slice: x: 4, y: 4 (y_hi: 2, y_lo: 2; y = y_hi * 2 + y_lo), z: 4, core: 2. Of those that a mesh axis runs over, the one named last changes fastest.
Arguments:
- voltages: bfloat16 [2, 512, 262144], P(None, 'stn', 'tm'), may hold values from -6 to 6
- delays: int32 [512], P('stn'), may hold values from 0 to 2048, as said below
- fringe: int32 [512], P('stn'), may hold values from 0 to 4095
- fringe_rate: int32 [512], P('stn'), may hold values from 0 to 4095
- filter_taps: float32 [16, 1024], replicated, may hold values from -1.5 to 1.5
Outputs:
- vis_real: float32 [1024, 512, 512], P(('stn', 'tm'))
- vis_imag: float32 [1024, 512, 512], P(('stn', 'tm'))
The draws below stay inside these ranges and needn't reach their ends.
Inputs may be any that keep to these rules, and one draw needn't show every extreme that they name: `delays`: the largest delay over all stations is exactly 2048.
All inputs are finite; a program needn't handle non-finite values.
Results may differ from the reference program's by a relative error of at most 0.0066.
Values may be sent and summed in bfloat16 or wider, within the bound.
No kernel may reach another device: no remote copies, remote signals or barrier semaphores. Data moves between devices by JAX's collectives and lax.ppermute only.
A program may use at most 192 MiB of HBM per device.

```python
import math
import jax
import jax.numpy as jnp
from jax import lax

S = 512
C = 1024
P_SIZE = 16
Q = 4096
TIME = 262144
DMAX = 2048


def draw_delays(key, part):
    key_values, key_place = jax.random.split(jax.random.fold_in(key, 7))
    values = jax.random.randint(key_values, (S,), 0, DMAX + 1)
    position = jax.random.randint(key_place, (), 0, S)
    return values.at[position].set(DMAX).astype(jnp.int32)


def set_ends(drawn, key, low, top_value):
    dims = drawn.shape
    spot = [jax.random.randint(jax.random.fold_in(key, axis), (), 0, dims[axis]) for axis in range(len(dims))]
    drawn = drawn.at[tuple(spot)].set(low)
    longest = dims.index(max(dims))
    spot[longest] = (spot[longest] + 1) % dims[longest]
    return drawn.at[tuple(spot)].set(top_value)


def levels(own_key, shape, cuts, least, high):
    loudness, own = 1.0, jax.random.fold_in(own_key, 6)
    for dim, shards_of in cuts:
        draws = jnp.exp(jax.random.uniform(jax.random.fold_in(own, dim), (shards_of,), jnp.float32, least / len(cuts), high / len(cuts)))
        loudness = loudness * jnp.repeat(draws, shape[dim] // shards_of).reshape([-1 if axis == dim else 1 for axis in range(len(shape))])
    return loudness


def scatter_about(own_key, dims, spread, most, cuts=(), kind=jnp.bfloat16):
    drawn = spread * jax.random.normal(own_key, dims, jnp.float32)
    if cuts:
        drawn = drawn * levels(own_key, dims, cuts, -0.22, 0.18)
    return jnp.clip(drawn, -most, most).astype(kind)


def setup_inputs(seed: int = 0) -> dict:
    key_list = jax.random.split(jax.random.key(seed), 6)
    voltages = scatter_about(key_list[0], (2, S, TIME), 1.0, 6.0, ((1, 32), (2, 4)))
    delays = draw_delays(jax.random.fold_in(key_list[5], 71), 0)
    fringe = set_ends(jax.random.randint(key_list[2], (S,), 0, Q), jax.random.fold_in(key_list[2], 1), 0, Q - 1).astype(jnp.int32)
    fringe_rate = set_ends(jax.random.randint(key_list[3], (S,), 0, Q), jax.random.fold_in(key_list[3], 1), 0, Q - 1).astype(jnp.int32)
    filter_taps = scatter_about(key_list[4], (P_SIZE, C), 0.25, 1.5, (), jnp.float32)
    return {"voltages": voltages, "delays": delays, "fringe": fringe, "fringe_rate": fringe_rate, "filter_taps": filter_taps}


TWO_PI = 2.0 * math.pi

def dft_tables(table_size):
    column = jnp.arange(table_size, dtype=jnp.int32)
    product = column[:, None] * column[None, :] % table_size
    angles = product.astype(jnp.float32) * (TWO_PI / table_size)
    return (jnp.cos(angles).astype(jnp.bfloat16), jnp.sin(angles).astype(jnp.bfloat16))

def transform(weighted_part, table):
    return jnp.einsum('smn,nc->csm', weighted_part.astype(jnp.float32), table.astype(jnp.float32), precision=lax.Precision.HIGHEST)

def channelize(delayed, filter_taps, fringe, fringe_rate, spectra, tables):
    stations = delayed.shape[1]
    blocks = delayed.reshape(2, stations, spectra + P_SIZE - 1, C)
    summed = jnp.zeros((2, stations, spectra, C), jnp.float32)
    for tap_index in range(P_SIZE):
        summed = summed + filter_taps[tap_index] * blocks[:, :, tap_index:tap_index + spectra].astype(jnp.float32)
    weighted = summed.astype(jnp.bfloat16)
    cosine_table, sine_table = tables
    inverse_root = 1.0 / math.sqrt(C)
    real_part = (transform(weighted[0], cosine_table) + transform(weighted[1], sine_table)) * inverse_root
    imag_part = (transform(weighted[1], cosine_table) - transform(weighted[0], sine_table)) * inverse_root
    channel = jnp.arange(C, dtype=jnp.int32)
    phase_index = (fringe[None, :] + fringe_rate[None, :] * channel[:, None]) % Q
    rotation = phase_index.astype(jnp.float32) * (TWO_PI / Q)
    rot_cos = jnp.cos(rotation)[:, :, None]
    rot_sin = jnp.sin(rotation)[:, :, None]
    out_real = real_part * rot_cos - imag_part * rot_sin
    out_imag = real_part * rot_sin + imag_part * rot_cos
    return jnp.stack([out_real, out_imag], axis=2).astype(jnp.bfloat16)

def reference(voltages, delays, fringe, fringe_rate, filter_taps):
    spectra = TIME // C
    padded = jnp.concatenate([jnp.zeros((2, S, DMAX), jnp.bfloat16), voltages, jnp.zeros((2, S, (P_SIZE - 1) * C), jnp.bfloat16)], axis=2)
    length = TIME + (P_SIZE - 1) * C
    tables = dft_tables(C)

    def select_window(station_row, delay_value):
        return lax.dynamic_slice_in_dim(station_row, (DMAX - delay_value).astype(jnp.int32), length, 1)

    def one_block(block_index):
        start = (block_index * 16).astype(jnp.int32)
        station_rows = lax.dynamic_slice_in_dim(padded, start, 16, 1)
        block_delays = lax.dynamic_slice_in_dim(delays, start, 16, 0)
        block_fringe = lax.dynamic_slice_in_dim(fringe, start, 16, 0)
        block_rate = lax.dynamic_slice_in_dim(fringe_rate, start, 16, 0)
        delayed = jax.vmap(select_window, in_axes=(1, 0), out_axes=1)(station_rows, block_delays)
        return channelize(delayed, filter_taps, block_fringe, block_rate, spectra, tables)
    stacked = lax.map(one_block, jnp.arange(S // 16, dtype=jnp.int32))

    def one_channel_block(block_index):
        start = (block_index * 8).astype(jnp.int32)
        chosen = lax.dynamic_slice_in_dim(stacked, start, 8, 1)
        left_rows = jnp.transpose(chosen, (1, 0, 2, 3, 4)).reshape(8, S, 2 * spectra).astype(jnp.float32)
        swapped = jnp.concatenate([left_rows[..., spectra:], -left_rows[..., :spectra]], axis=-1)
        gram_real = jnp.einsum('csk,cdk->csd', left_rows, left_rows, precision=lax.Precision.HIGHEST)
        gram_imag = jnp.einsum('csk,cdk->csd', swapped, left_rows, precision=lax.Precision.HIGHEST)
        return (gram_real * (1.0 / spectra), gram_imag * (1.0 / spectra))
    vis_real, vis_imag = lax.map(one_channel_block, jnp.arange(C // 8, dtype=jnp.int32))
    return (vis_real.reshape(C, S, S), vis_imag.reshape(C, S, S))
```

```python
import math

import jax
import jax.numpy as jnp
import numpy as np
from jax import lax
from jax.experimental import pallas as pl
from jax.experimental.pallas import tpu as pltpu
from jax.sharding import PartitionSpec as P

C = 1024
P_SIZE = 16
Q = 4096
DMAX = 2048
LANES = 128
SUB = 8
RADIX = 4
K = C // RADIX
TWO_PI = 2.0 * math.pi
BF16 = jnp.bfloat16
F32 = jnp.float32


def from_behind(block, axis, distance):
    devices = range(lax.axis_size(axis))
    route = [(i - distance, i) for i in devices if i - distance in devices]
    return lax.ppermute(block, axis, route)


def dft_table():
    channel = (RADIX * np.arange(K)[None, :] + np.arange(RADIX)[:, None]).reshape(C)
    angle = (channel[:, None] * np.arange(K)[None, :] % C) * (TWO_PI / C)
    return np.concatenate([np.cos(angle), np.sin(angle)], axis=1).astype(BF16)


def rotation_tables(fringe, fringe_rate):
    channel = (RADIX * jnp.arange(K)[None, :] + jnp.arange(RADIX)[:, None]).reshape(C)
    phase = (fringe[None, :] + fringe_rate[None, :] * channel[:, None]) % Q
    angle = phase.astype(F32) * (TWO_PI / Q)
    scale = 1.0 / math.sqrt(C)
    return jnp.cos(angle) * scale, jnp.sin(angle) * scale


EARLY = DMAX // LANES
LATE = (P_SIZE - 1) * C // LANES
ROW_PAD = 8


def front_kernel(
    delays, volts, early, late, taps, table, rot_cos, rot_sin, out, lin, filt, zs, turned
):
    stations, samples = volts.shape[1], volts.shape[2]
    frames = samples // C
    blocks = samples // LANES
    row_step = lin.shape[0] // (2 * stations)

    def spread(source, count, offset, unroll):
        def body(step, carry):
            for inner in range(unroll):
                block = step * unroll + inner
                lanes = pl.ds(pl.multiple_of(block * LANES, LANES), LANES)
                for part in range(2):
                    tile = source[part, :, lanes].astype(F32)
                    for top in range(0, stations, SUB):
                        start = (part * stations + top) * row_step + ROW_PAD + offset + block
                        lin[pl.ds(start, SUB, stride=row_step), :] = tile[top : top + SUB]
            return carry

        lax.fori_loop(0, count // unroll, body, 0)

    spread(early, EARLY, 0, 8)
    spread(volts, blocks, EARLY, 8)
    spread(late, LATE, EARLY + blocks, 8)

    lane = lax.broadcasted_iota(jnp.int32, (SUB, LANES), 1)

    def filter_row(row, carry):
        delay = delays[row % stations]
        shift = delay % LANES
        base = row * row_step + ROW_PAD + EARLY - delay // LANES
        keep = lane < LANES - shift
        sums = {}
        for k in range(frames + P_SIZE - 1):
            here = lin[pl.ds(base + SUB * k, SUB), :]
            before = lin[pl.ds(base + SUB * k - 1, SUB), :]
            frame = pltpu.roll(jnp.where(keep, here, before), shift, 1)
            for p in range(P_SIZE):
                m = k - p
                if 0 <= m < frames:
                    term = taps[SUB * p : SUB * (p + 1), :] * frame
                    sums[m] = sums[m] + term if m in sums else term
            m = k - (P_SIZE - 1)
            if m >= 0:
                start = pl.multiple_of(row * (frames * SUB), SUB) + m * SUB
                filt[pl.ds(start, SUB), :] = sums.pop(m)
        return carry

    lax.fori_loop(0, 2 * stations, filter_row, 0)

    def butterflies(s, carry):
        def load(part, j):
            start = (part * stations + s) * (frames * SUB) + j
            return filt[pl.ds(start, frames, stride=SUB), :]

        for half in range(2):
            re = [load(0, 2 * q + half) for q in range(4)]
            im = [load(1, 2 * q + half) for q in range(4)]
            re_e, re_d = re[0] + re[2], re[0] - re[2]
            im_e, im_d = im[0] + im[2], im[0] - im[2]
            re_f, re_g = re[1] + re[3], re[1] - re[3]
            im_f, im_g = im[1] + im[3], im[1] - im[3]
            z = [
                (re_e + re_f, im_e + im_f),
                (re_d + im_g, im_d - re_g),
                (re_e - re_f, im_e - im_f),
                (re_d - im_g, im_d + re_g),
            ]
            for r in range(RADIX):
                zr, zi = z[r][0].astype(BF16), z[r][1].astype(BF16)
                top = pl.multiple_of(s * 2 * frames, 2 * frames)
                cols = pl.ds(half * LANES, LANES)
                cols_sin = pl.ds(K + half * LANES, LANES)
                zs[r, pl.ds(top, frames), cols] = zr
                zs[r, pl.ds(top, frames), cols_sin] = zi
                zs[r, pl.ds(top + frames, frames), cols] = zi
                zs[r, pl.ds(top + frames, frames), cols_sin] = -zr
        return carry

    lax.fori_loop(0, stations, butterflies, 0)

    width = 2 * frames
    sign = jnp.where(lax.broadcasted_iota(jnp.int32, (1, width), 1) < frames, -1.0, 1.0)

    def transform(r, carry):
        rows = pl.ds(pl.multiple_of(r * K, K), K)
        weights = table[rows, :]
        cosines = rot_cos[rows, :]
        sines = rot_sin[rows, :]
        for s0 in range(0, stations, 2):
            both = lax.dot_general(
                weights,
                zs[r, s0 * width : (s0 + 2) * width, :],
                (((1,), (1,)), ((), ())),
                preferred_element_type=F32,
            )
            for s in (s0, s0 + 1):
                spec = both[:, (s - s0) * width : (s - s0 + 1) * width]
                cross = pltpu.roll(spec, frames, 1) * sign
                rotated = spec * cosines[:, s : s + 1] + cross * sines[:, s : s + 1]
                turned[pl.ds(s, K, stride=stations), :] = rotated
        for k0 in range(0, K, 16):
            piece = turned[k0 * stations : (k0 + 16) * stations, :].astype(BF16)
            out[k0 : k0 + 16, r] = piece.reshape(16, stations, width)
        return carry

    lax.fori_loop(0, RADIX, transform, 0)


def front(delays, voltages, early, late, filter_taps, fringe, fringe_rate):
    stations, samples = voltages.shape[1], voltages.shape[2]
    frames = samples // C
    blocks = samples // LANES
    row_step = ROW_PAD + EARLY + blocks + LATE + 1
    rot_cos, rot_sin = rotation_tables(fringe, fringe_rate)
    taps = filter_taps.reshape(P_SIZE * SUB, LANES)
    vmem = pl.BlockSpec(memory_space=pltpu.VMEM)
    smem = pl.BlockSpec(memory_space=pltpu.SMEM)
    return pl.pallas_call(
        front_kernel,
        out_shape=jax.ShapeDtypeStruct((K, RADIX, stations, 2 * frames), BF16),
        in_specs=[smem] + [vmem] * 7,
        out_specs=vmem,
        scratch_shapes=[
            pltpu.VMEM((-(-(2 * stations * row_step) // 8) * 8, LANES), F32),
            pltpu.VMEM((2 * stations * frames * SUB, LANES), F32),
            pltpu.VMEM((RADIX, stations * 2 * frames, 2 * K), BF16),
            pltpu.VMEM((K * stations, LANES), F32),
        ],
        compiler_params=pltpu.CompilerParams(vmem_limit_bytes=56 * 1024 * 1024),
        name="front",
    )(delays, voltages, early, late, taps, jnp.asarray(dft_table()), rot_cos, rot_sin)


def gram_kernel(scale, groups, times, received, real, imag):
    stations, width = received.shape[1], received.shape[2]
    half = width // 2
    tiles = received[...].reshape(groups, times, stations, width)
    direct, swapped = [], []
    for t in range(times):
        tile = tiles[:, t].reshape(groups * stations, width)
        direct.append(tile)
        swapped.append(jnp.concatenate([tile[:, half:], -tile[:, :half]], axis=1))
    rows = jnp.concatenate(direct, axis=1)
    turned_rows = jnp.concatenate(swapped, axis=1)
    contract = (((1,), (1,)), ((), ()))
    real[0] = lax.dot_general(rows, rows, contract, preferred_element_type=F32) * scale
    imag[0] = lax.dot_general(turned_rows, rows, contract, preferred_element_type=F32) * scale


def gram(received, groups, times):
    devices, channels, stations, width = received.shape
    whole = groups * stations
    scale = 1.0 / (times * width // 2)
    shape = jax.ShapeDtypeStruct((channels, whole, whole), F32)
    block = pl.BlockSpec((1, whole, whole), lambda c: (c, 0, 0))

    def body(received, real, imag):
        gram_kernel(scale, groups, times, received, real, imag)

    return pl.pallas_call(
        body,
        grid=(channels,),
        out_shape=(shape, shape),
        in_specs=[pl.BlockSpec((devices, None, stations, width), lambda c: (0, c, 0, 0))],
        out_specs=(block, block),
        compiler_params=pltpu.CompilerParams(vmem_limit_bytes=48 * 1024 * 1024),
        name="gram",
    )(received)


def local(voltages, delays, fringe, fringe_rate, filter_taps):
    samples = voltages.shape[2]
    stations = voltages.shape[1]
    frames = samples // C
    early = from_behind(voltages[:, :, samples - DMAX :], "tm", 1)
    late = from_behind(voltages[:, :, : (P_SIZE - 1) * C], "tm", -1)
    turned = front(delays, voltages, early, late, filter_taps, fringe, fringe_rate)
    groups, times = lax.axis_size("stn"), lax.axis_size("tm")
    devices = groups * times
    outgoing = turned.reshape(devices, C // devices, stations, 2 * frames)
    received = lax.all_to_all(outgoing, ("stn", "tm"), split_axis=0, concat_axis=0, tiled=True)
    return gram(received, groups, times)


def solution(mesh):
    return jax.shard_map(
        local,
        mesh=mesh,
        in_specs=(P(None, "stn", "tm"), P("stn"), P("stn"), P("stn"), P()),
        out_specs=(P(("stn", "tm"), None, None), P(("stn", "tm"), None, None)),
        check_vma=False,
    )
```

```python
import math

import jax
import jax.numpy as jnp
import numpy as np
from jax import lax
from jax.experimental import pallas as pl
from jax.experimental.pallas import tpu as pltpu
from jax.sharding import PartitionSpec as P

C = 1024
P_SIZE = 16
Q = 4096
DMAX = 2048
LANES = 128
SUB = 8
RADIX = 4
K = C // RADIX
TWO_PI = 2.0 * math.pi
BF16 = jnp.bfloat16
F32 = jnp.float32


def from_behind(block, axis, distance):
    devices = range(lax.axis_size(axis))
    route = [(i - distance, i) for i in devices if i - distance in devices]
    return lax.ppermute(block, axis, route)


def dft_table():
    channel = (RADIX * np.arange(K)[None, :] + np.arange(RADIX)[:, None]).reshape(C)
    angle = (channel[:, None] * np.arange(K)[None, :] % C) * (TWO_PI / C)
    return np.concatenate([np.cos(angle), np.sin(angle)], axis=1).astype(BF16)


def rotation_tables(fringe, fringe_rate):
    fine = (fringe[:, None] + fringe_rate[:, None] * jnp.arange(RADIX)[None, :]) % Q
    fine = fine.astype(F32) * (TWO_PI / Q)
    scale = 1.0 / math.sqrt(C)
    phases = jnp.stack([jnp.cos(fine) * scale, jnp.sin(fine) * scale], axis=2).reshape(-1)
    coarse = (RADIX * fringe_rate[:, None] * jnp.arange(K)[None, :]) % Q
    coarse = coarse.astype(F32) * (TWO_PI / Q)
    coarse = lax.optimization_barrier(jnp.concatenate([jnp.cos(coarse), jnp.sin(coarse)]))
    return phases, coarse.T


EARLY = DMAX // LANES
LATE = (P_SIZE - 1) * C // LANES
ROW_PAD = 8
STEP = SUB + 1


def spread(source, first, count, offset, stations, row_step, lin):
    unroll = 8

    def body(step, carry):
        for inner in range(unroll):
            block = step * unroll + inner
            lanes = pl.ds(pl.multiple_of((first + block) * LANES, LANES), LANES)
            for part in range(2):
                tile = source[part, :, lanes].astype(F32)
                for top in range(0, stations, SUB):
                    start = (part * stations + top) * row_step + ROW_PAD + offset + block
                    lin[pl.ds(start, SUB, stride=row_step), :] = tile[top : top + SUB]
        return carry

    lax.fori_loop(0, count // unroll, body, 0)


def filter_frames(delays, taps, stations, frames, row_step, lin, filt):
    lane = lax.broadcasted_iota(jnp.int32, (SUB, LANES), 1)

    def filter_row(row, carry):
        delay = delays[row % stations]
        shift = delay % LANES
        base = row * row_step + ROW_PAD + EARLY - delay // LANES
        keep = lane < LANES - shift
        sums = {}
        for k in range(frames + P_SIZE - 1):
            here = lin[pl.ds(base + SUB * k, SUB), :]
            before = lin[pl.ds(base + SUB * k - 1, SUB), :]
            frame = pltpu.roll(jnp.where(keep, here, before), shift, 1)
            for p in range(P_SIZE):
                m = k - p
                if 0 <= m < frames:
                    term = taps[SUB * p : SUB * (p + 1), :] * frame
                    sums[m] = sums[m] + term if m in sums else term
            m = k - (P_SIZE - 1)
            if m >= 0:
                filt[pl.ds((row * frames + m) * STEP, SUB), :] = sums.pop(m)
        return carry

    lax.fori_loop(0, 2 * stations, filter_row, 0, unroll=2)


def butterflies(phases, stations, frames, filt, zs):
    def body(s, carry):
        def load(part, j):
            start = (part * stations + s) * (frames * STEP) + j
            return filt[pl.ds(start, frames, stride=STEP), :]

        for half in range(2):
            re = [load(0, 2 * q + half) for q in range(4)]
            im = [load(1, 2 * q + half) for q in range(4)]
            re_e, re_d = re[0] + re[2], re[0] - re[2]
            im_e, im_d = im[0] + im[2], im[0] - im[2]
            re_f, re_g = re[1] + re[3], re[1] - re[3]
            im_f, im_g = im[1] + im[3], im[1] - im[3]
            z = [
                (re_e + re_f, im_e + im_f),
                (re_d + im_g, im_d - re_g),
                (re_e - re_f, im_e - im_f),
                (re_d - im_g, im_d + re_g),
            ]
            for r in range(RADIX):
                cosine = phases[(s * RADIX + r) * 2]
                sine = phases[(s * RADIX + r) * 2 + 1]
                zr = z[r][0] * cosine - z[r][1] * sine
                zi = z[r][0] * sine + z[r][1] * cosine
                zs[r, s, :, pl.ds(half * LANES, LANES)] = zr.astype(BF16)
                zs[r, s, :, pl.ds(K + half * LANES, LANES)] = zi.astype(BF16)
        return carry

    lax.fori_loop(0, stations, body, 0)


def first_kernel(delays, phases, volts, early, taps, zs, lin, filt):
    stations, samples = volts.shape[1], volts.shape[2]
    frames = zs.shape[2]
    row_step = lin.shape[0] // (2 * stations)
    spread(early, 0, EARLY, 0, stations, row_step, lin)
    spread(volts, 0, samples // LANES, EARLY, stations, row_step, lin)
    filter_frames(delays, taps, stations, frames, row_step, lin, filt)
    butterflies(phases, stations, frames, filt, zs)


def second_kernel(
    delays, phases, volts, late, taps, table, coarse, before, out,
    lin, filt, zs, cosines, sines, turned, packed, sems
):
    stations = volts.shape[1]
    done, frames = before.shape[2], zs.shape[2]
    width = 2 * (done + frames)
    row_step = lin.shape[0] // (2 * stations)
    sign = jnp.where(lax.broadcasted_iota(jnp.int32, (1, width), 1) < width // 2, -1.0, 1.0)
    for s in range(stations):
        rows = slice(s * K, (s + 1) * K)
        cosines[rows, :] = jnp.broadcast_to(coarse[:, s : s + 1], (K, width))
        sines[rows, :] = coarse[:, stations + s : stations + s + 1] * sign
    blocks = frames * C // LANES + EARLY
    spread(volts, volts.shape[2] // LANES - blocks, blocks, 0, stations, row_step, lin)
    spread(late, 0, LATE, blocks, stations, row_step, lin)
    filter_frames(delays, taps, stations, frames, row_step, lin, filt)
    butterflies(phases, stations, frames, filt, zs)

    def sent(r, slot):
        return pltpu.make_async_copy(packed.at[slot], out.at[:, r], sems.at[slot])

    for r in range(RADIX):
        slot = r % 2
        weights = table[r * K : (r + 1) * K, :]
        for s0 in range(0, stations, 2):
            sides = []
            for s in (s0, s0 + 1):
                z = jnp.concatenate([before[r, s], zs[r, s]], axis=0)
                sides += [z, jnp.concatenate([z[:, K:], -z[:, :K]], axis=1)]
            both = lax.dot_general(
                weights,
                jnp.concatenate(sides, axis=0),
                (((1,), (1,)), ((), ())),
                preferred_element_type=F32,
            )
            for s in (s0, s0 + 1):
                rows = slice(s * K, (s + 1) * K)
                spec = both[:, (s - s0) * width : (s - s0 + 1) * width]
                cross = pltpu.roll(spec, width // 2, 1)
                rotated = spec * cosines[rows, :] + cross * sines[rows, :]
                turned[pl.ds(s, K, stride=stations + 1), :] = rotated
        if r >= 2:
            sent(r - 2, slot).wait()
        for k in range(K):
            top = k * (stations + 1)
            packed[slot, k] = turned[top : top + stations, :].astype(BF16)
        sent(r, slot).start()
    sent(RADIX - 2, 0).wait()
    sent(RADIX - 1, 1).wait()


def rows_of(count):
    return -(-count // SUB) * SUB


def front(delays, voltages, early, late, filter_taps, fringe, fringe_rate):
    stations, samples = voltages.shape[1], voltages.shape[2]
    frames = samples // C
    ahead = P_SIZE * (frames // P_SIZE - 1)
    rest = frames - ahead
    phases, coarse = rotation_tables(fringe, fringe_rate)
    taps = filter_taps.reshape(P_SIZE * SUB, LANES)
    vmem = pl.BlockSpec(memory_space=pltpu.VMEM)
    smem = pl.BlockSpec(memory_space=pltpu.SMEM)
    anywhere = pl.BlockSpec(memory_space=pl.ANY)
    step = ROW_PAD + EARLY + samples // LANES + 1
    first = pl.pallas_call(
        first_kernel,
        out_shape=jax.ShapeDtypeStruct((RADIX, stations, ahead, 2 * K), BF16),
        in_specs=[smem, smem, vmem, vmem, vmem],
        out_specs=vmem,
        scratch_shapes=[
            pltpu.VMEM((rows_of(2 * stations * step), LANES), F32),
            pltpu.VMEM((2 * stations * ahead * STEP, LANES), F32),
        ],
        compiler_params=pltpu.CompilerParams(vmem_limit_bytes=36 * 2**20),
        cost_estimate=pl.CostEstimate(
            flops=10**10, bytes_accessed=2**23, transcendentals=0
        ),
        name="first",
    )(delays, phases, voltages, early, taps)
    tail = rest * C + DMAX
    step = ROW_PAD + tail // LANES + LATE + 1
    return pl.pallas_call(
        second_kernel,
        out_shape=jax.ShapeDtypeStruct((K, RADIX, stations, 2 * frames), BF16),
        in_specs=[smem, smem, vmem, vmem, vmem, vmem, vmem, vmem],
        out_specs=anywhere,
        scratch_shapes=[
            pltpu.VMEM((rows_of(2 * stations * step), LANES), F32),
            pltpu.VMEM((2 * stations * rest * STEP, LANES), F32),
            pltpu.VMEM((RADIX, stations, rest, 2 * K), BF16),
            pltpu.VMEM((stations * K, 2 * frames), F32),
            pltpu.VMEM((stations * K, 2 * frames), F32),
            pltpu.VMEM((K * (stations + 1), 2 * frames), F32),
            pltpu.VMEM((2, K, stations, 2 * frames), BF16),
            pltpu.SemaphoreType.DMA((2,)),
        ],
        compiler_params=pltpu.CompilerParams(vmem_limit_bytes=40 * 2**20),
        cost_estimate=pl.CostEstimate(
            flops=10**10, bytes_accessed=2**23, transcendentals=0
        ),
        name="second",
    )(delays, phases, voltages, late, taps, jnp.asarray(dft_table()), coarse, first)


def gram_kernel(scale, groups, times, received, real, imag):
    stations, width = received.shape[1], received.shape[2]
    half = width // 2
    tiles = received[...].reshape(groups, times, stations, width)
    direct, swapped = [], []
    for t in range(times):
        tile = tiles[:, t].reshape(groups * stations, width)
        direct.append(tile)
        swapped.append(jnp.concatenate([tile[:, half:], -tile[:, :half]], axis=1))
    rows = jnp.concatenate(direct, axis=1)
    turned_rows = jnp.concatenate(swapped, axis=1)
    contract = (((1,), (1,)), ((), ()))
    real[0] = lax.dot_general(rows, rows, contract, preferred_element_type=F32) * scale
    imag[0] = lax.dot_general(turned_rows, rows, contract, preferred_element_type=F32) * scale


def gram(received, groups, times):
    devices, channels, stations, width = received.shape
    whole = groups * stations
    scale = 1.0 / (times * width // 2)
    shape = jax.ShapeDtypeStruct((channels, whole, whole), F32)
    block = pl.BlockSpec((1, whole, whole), lambda c: (c, 0, 0))

    def body(received, real, imag):
        gram_kernel(scale, groups, times, received, real, imag)

    return pl.pallas_call(
        body,
        grid=(channels,),
        out_shape=(shape, shape),
        in_specs=[pl.BlockSpec((devices, None, stations, width), lambda c: (0, c, 0, 0))],
        out_specs=(block, block),
        compiler_params=pltpu.CompilerParams(vmem_limit_bytes=48 * 1024 * 1024),
        name="gram",
    )(received)


def local(voltages, delays, fringe, fringe_rate, filter_taps):
    samples = voltages.shape[2]
    stations = voltages.shape[1]
    frames = samples // C
    early = from_behind(voltages[:, :, samples - DMAX :], "tm", 1)
    late = from_behind(voltages[:, :, : (P_SIZE - 1) * C], "tm", -1)
    turned = front(delays, voltages, early, late, filter_taps, fringe, fringe_rate)
    groups, times = lax.axis_size("stn"), lax.axis_size("tm")
    devices = groups * times
    outgoing = turned.reshape(devices, C // devices, stations, 2 * frames)
    received = lax.all_to_all(outgoing, ("stn", "tm"), split_axis=0, concat_axis=0, tiled=True)
    return gram(received, groups, times)


def solution(mesh):
    return jax.shard_map(
        local,
        mesh=mesh,
        in_specs=(P(None, "stn", "tm"), P("stn"), P("stn"), P("stn"), P()),
        out_specs=(P(("stn", "tm"), None, None), P(("stn", "tm"), None, None)),
        check_vma=False,
    )
```

```python
import math

import jax
import jax.numpy as jnp
import numpy as np
from jax import lax
from jax.experimental import pallas as pl
from jax.experimental.pallas import tpu as pltpu
from jax.sharding import PartitionSpec as P

C = 1024
P_SIZE = 16
Q = 4096
DMAX = 2048
LANES = 128
SUB = 8
RADIX = 4
K = C // RADIX
TWO_PI = 2.0 * math.pi
BF16 = jnp.bfloat16
F32 = jnp.float32


def from_behind(block, axis, distance):
    devices = range(lax.axis_size(axis))
    route = [(i - distance, i) for i in devices if i - distance in devices]
    return lax.ppermute(block, axis, route)


def dft_table():
    channel = (RADIX * np.arange(K)[None, :] + np.arange(RADIX)[:, None]).reshape(C)
    angle = (channel[:, None] * np.arange(K)[None, :] % C) * (TWO_PI / C)
    return np.concatenate([np.cos(angle), np.sin(angle)], axis=1).astype(BF16)


EARLY = DMAX // LANES
LATE = (P_SIZE - 1) * C // LANES
ROW_PAD = 8
STEP = SUB + 1


def phase_rows(fringe, fringe_rate, stations, phases):
    row = lax.broadcasted_iota(jnp.int32, (SUB, LANES), 0)
    turn = (row & 1).astype(F32) * (math.pi / 2)
    for s in range(stations):
        phase = (fringe[s] + fringe_rate[s] * (row >> 1)) & (Q - 1)
        angle = phase.astype(F32) * (TWO_PI / Q) - turn
        phases[s * SUB : (s + 1) * SUB, :] = jnp.cos(angle) * (1.0 / math.sqrt(C))


def coarse_columns(fringe_rate, stations):
    row = lax.broadcasted_iota(jnp.int32, (2 * stations, K), 0)
    k = lax.broadcasted_iota(jnp.int32, (2 * stations, K), 1)
    rate = jnp.zeros((2 * stations, K), jnp.int32)
    for s in range(stations):
        rate = jnp.where(row % stations == s, fringe_rate[s], rate)
    angle = ((RADIX * rate * k) & (Q - 1)).astype(F32) * (TWO_PI / Q)
    values = jnp.cos(angle - jnp.where(row < stations, 0.0, math.pi / 2))
    padding = jnp.zeros((LANES - 2 * stations, K), F32)
    return jnp.concatenate([values, padding], axis=0).T


def tap_rows(filter_taps, taps):
    for p in range(P_SIZE):
        for j in range(SUB):
            row = p * SUB + j
            taps[row : row + 1, :] = filter_taps[p : p + 1, j * LANES : (j + 1) * LANES]


def spread(source, first, count, offset, stations, row_step, lin):
    unroll = 8

    def body(step, carry):
        for inner in range(unroll):
            block = step * unroll + inner
            lanes = pl.ds(pl.multiple_of((first + block) * LANES, LANES), LANES)
            for part in range(2):
                tile = source[part, :, lanes].astype(F32)
                for top in range(0, stations, SUB):
                    start = (part * stations + top) * row_step + ROW_PAD + offset + block
                    lin[pl.ds(start, SUB, stride=row_step), :] = tile[top : top + SUB]
        return carry

    lax.fori_loop(0, count // unroll, body, 0)


def filter_frames(delays, taps, stations, frames, row_step, lin, filt):
    lane = lax.broadcasted_iota(jnp.int32, (SUB, LANES), 1)

    def filter_row(row, carry):
        delay = delays[row % stations]
        shift = delay % LANES
        base = row * row_step + ROW_PAD + EARLY - delay // LANES
        keep = lane < LANES - shift
        sums = {}
        for k in range(frames + P_SIZE - 1):
            here = lin[pl.ds(base + SUB * k, SUB), :]
            before = lin[pl.ds(base + SUB * k - 1, SUB), :]
            frame = pltpu.roll(jnp.where(keep, here, before), shift, 1)
            for p in range(P_SIZE):
                m = k - p
                if 0 <= m < frames:
                    term = taps[SUB * p : SUB * (p + 1), :] * frame
                    sums[m] = sums[m] + term if m in sums else term
            m = k - (P_SIZE - 1)
            if m >= 0:
                filt[pl.ds((row * frames + m) * STEP, SUB), :] = sums.pop(m)
        return carry

    lax.fori_loop(0, 2 * stations, filter_row, 0, unroll=2)


def butterflies(phases, stations, frames, filt, zs, top=0):
    def body(s, carry):
        def load(part, j):
            start = (part * stations + s) * (frames * STEP) + j
            return filt[pl.ds(start, frames, stride=STEP), :]

        for half in range(2):
            re = [load(0, 2 * q + half) for q in range(4)]
            im = [load(1, 2 * q + half) for q in range(4)]
            re_e, re_d = re[0] + re[2], re[0] - re[2]
            im_e, im_d = im[0] + im[2], im[0] - im[2]
            re_f, re_g = re[1] + re[3], re[1] - re[3]
            im_f, im_g = im[1] + im[3], im[1] - im[3]
            z = [
                (re_e + re_f, im_e + im_f),
                (re_d + im_g, im_d - re_g),
                (re_e - re_f, im_e - im_f),
                (re_d - im_g, im_d + re_g),
            ]
            for r in range(RADIX):
                cosine = phases[pl.ds(s * SUB + 2 * r, 1), :]
                sine = phases[pl.ds(s * SUB + 2 * r + 1, 1), :]
                zr = z[r][0] * cosine - z[r][1] * sine
                zi = z[r][0] * sine + z[r][1] * cosine
                zs[r, s, top : top + frames, pl.ds(half * LANES, LANES)] = zr.astype(BF16)
                zs[r, s, top : top + frames, pl.ds(K + half * LANES, LANES)] = zi.astype(BF16)
        return carry

    lax.fori_loop(0, stations, body, 0)


def rims_kernel(volts, early, late, sems):
    samples = volts.shape[2]
    size = early.shape[2]
    copies = [
        pltpu.make_async_copy(
            volts.at[:, :, pl.ds(0, late.shape[2])], late, sems.at[0]
        ),
        pltpu.make_async_copy(
            volts.at[:, :, pl.ds(samples - size, size)], early, sems.at[1]
        ),
    ]
    for copy in copies:
        copy.start()
    for copy in copies:
        copy.wait()


def first_kernel(
    delays, fringe, fringe_rate, volts, filter_taps, zs, phases, coarse, taps, lin, filt
):
    stations = volts.shape[1]
    frames = zs.shape[2]
    row_step = lin.shape[0] // (2 * stations)
    phase_rows(fringe, fringe_rate, stations, phases)
    coarse[...] = coarse_columns(fringe_rate, stations)
    tap_rows(filter_taps, taps)
    blocks = (frames + P_SIZE - 1) * SUB + EARLY
    spread(volts, P_SIZE * SUB - EARLY, blocks, 0, stations, row_step, lin)
    filter_frames(delays, taps, stations, frames, row_step, lin, filt)
    butterflies(phases, stations, frames, filt, zs)


def second_kernel(
    delays, volts, early, late, taps, table, phases, coarse, before, out,
    lin, filt, zs, cosines, sines, turned, packed, sems
):
    stations, blocks = volts.shape[1], volts.shape[2] // LANES
    frames = zs.shape[2]
    width = 2 * (before.shape[2] + frames)
    row_step = lin.shape[0] // (2 * stations)
    sign = jnp.where(lax.broadcasted_iota(jnp.int32, (1, width), 1) < width // 2, -1.0, 1.0)
    for s in range(stations):
        rows = slice(s * K, (s + 1) * K)
        cosines[rows, :] = jnp.broadcast_to(coarse[:, s : s + 1], (K, width))
        sines[rows, :] = coarse[:, stations + s : stations + s + 1] * sign
    spread(early, 0, EARLY, 0, stations, row_step, lin)
    spread(volts, 0, (2 * P_SIZE - 1) * SUB, EARLY, stations, row_step, lin)
    filter_frames(delays, taps, stations, P_SIZE, row_step, lin, filt)
    butterflies(phases, stations, P_SIZE, filt, zs)
    own = P_SIZE * SUB + EARLY
    spread(volts, blocks - own, own, 0, stations, row_step, lin)
    spread(late, 0, LATE, own, stations, row_step, lin)
    filter_frames(delays, taps, stations, P_SIZE, row_step, lin, filt)
    butterflies(phases, stations, P_SIZE, filt, zs, P_SIZE)

    def sent(r, slot):
        return pltpu.make_async_copy(packed.at[slot], out.at[:, r], sems.at[slot])

    for r in range(RADIX):
        slot = r % 2
        weights = table[r * K : (r + 1) * K, :]
        for s0 in range(0, stations, 2):
            sides = []
            for s in (s0, s0 + 1):
                z = jnp.concatenate([before[r, s], zs[r, s]], axis=0)
                sides += [z, jnp.concatenate([z[:, K:], -z[:, :K]], axis=1)]
            both = lax.dot_general(
                weights,
                jnp.concatenate(sides, axis=0),
                (((1,), (1,)), ((), ())),
                preferred_element_type=F32,
            )
            for s in (s0, s0 + 1):
                rows = slice(s * K, (s + 1) * K)
                spec = both[:, (s - s0) * width : (s - s0 + 1) * width]
                cross = pltpu.roll(spec, width // 2, 1)
                rotated = spec * cosines[rows, :] + cross * sines[rows, :]
                turned[pl.ds(s, K, stride=stations + 1), :] = rotated
        if r >= 2:
            sent(r - 2, slot).wait()
        for k in range(K):
            top = k * (stations + 1)
            packed[slot, k] = turned[top : top + stations, :].astype(BF16)
        sent(r, slot).start()
    sent(RADIX - 2, 0).wait()
    sent(RADIX - 1, 1).wait()


def rows_of(count):
    return -(-count // SUB) * SUB


def front(voltages, delays, fringe, fringe_rate, filter_taps):
    stations, samples = voltages.shape[1], voltages.shape[2]
    frames = samples // C
    rest = 2 * P_SIZE
    ahead = frames - rest
    vmem = pl.BlockSpec(memory_space=pltpu.VMEM)
    smem = pl.BlockSpec(memory_space=pltpu.SMEM)
    anywhere = pl.BlockSpec(memory_space=pl.ANY)
    estimate = pl.CostEstimate(flops=10**10, bytes_accessed=2**23, transcendentals=0)
    early, late = pl.pallas_call(
        rims_kernel,
        out_shape=[
            jax.ShapeDtypeStruct((2, stations, DMAX), BF16),
            jax.ShapeDtypeStruct((2, stations, (P_SIZE - 1) * C), BF16),
        ],
        in_specs=[anywhere],
        out_specs=[vmem, vmem],
        scratch_shapes=[pltpu.SemaphoreType.DMA((2,))],
        compiler_params=pltpu.CompilerParams(vmem_limit_bytes=57 * 2**20),
        name="rims",
    )(voltages)
    late = from_behind(late, "tm", -1)
    early = from_behind(early, "tm", 1)
    step = ROW_PAD + EARLY + (ahead + P_SIZE - 1) * SUB + 1
    before, phases, coarse, taps = pl.pallas_call(
        first_kernel,
        out_shape=[
            jax.ShapeDtypeStruct((RADIX, stations, ahead, 2 * K), BF16),
            jax.ShapeDtypeStruct((stations * SUB, LANES), F32),
            jax.ShapeDtypeStruct((K, LANES), F32),
            jax.ShapeDtypeStruct((P_SIZE * SUB, LANES), F32),
        ],
        in_specs=[smem, smem, smem, vmem, vmem],
        out_specs=[vmem] * 4,
        scratch_shapes=[
            pltpu.VMEM((rows_of(2 * stations * step), LANES), F32),
            pltpu.VMEM((2 * stations * ahead * STEP, LANES), F32),
        ],
        compiler_params=pltpu.CompilerParams(vmem_limit_bytes=28 * 2**20),
        cost_estimate=estimate,
        name="first",
    )(delays, fringe, fringe_rate, voltages, filter_taps)
    step = ROW_PAD + EARLY + (2 * P_SIZE - 1) * SUB + 1
    return pl.pallas_call(
        second_kernel,
        out_shape=jax.ShapeDtypeStruct((K, RADIX, stations, 2 * frames), BF16),
        in_specs=[smem] + [vmem] * 8,
        out_specs=anywhere,
        scratch_shapes=[
            pltpu.VMEM((rows_of(2 * stations * step), LANES), F32),
            pltpu.VMEM((2 * stations * P_SIZE * STEP, LANES), F32),
            pltpu.VMEM((RADIX, stations, rest, 2 * K), BF16),
            pltpu.VMEM((stations * K, 2 * frames), F32),
            pltpu.VMEM((stations * K, 2 * frames), F32),
            pltpu.VMEM((K * (stations + 1), 2 * frames), F32),
            pltpu.VMEM((2, K, stations, 2 * frames), BF16),
            pltpu.SemaphoreType.DMA((2,)),
        ],
        compiler_params=pltpu.CompilerParams(vmem_limit_bytes=40 * 2**20),
        cost_estimate=estimate,
        name="second",
    )(
        delays, voltages, early, late, taps, jnp.asarray(dft_table()), phases, coarse, before
    )


def gram_kernel(scale, groups, times, received, real, imag):
    stations, width = received.shape[1], received.shape[2]
    half = width // 2
    tiles = received[...].reshape(groups, times, stations, width)
    direct, swapped = [], []
    for t in range(times):
        tile = tiles[:, t].reshape(groups * stations, width)
        direct.append(tile)
        swapped.append(jnp.concatenate([tile[:, half:], -tile[:, :half]], axis=1))
    rows = jnp.concatenate(direct, axis=1)
    turned_rows = jnp.concatenate(swapped, axis=1)
    contract = (((1,), (1,)), ((), ()))
    real[0] = lax.dot_general(rows, rows, contract, preferred_element_type=F32) * scale
    imag[0] = lax.dot_general(turned_rows, rows, contract, preferred_element_type=F32) * scale


def gram(received, groups, times):
    devices, channels, stations, width = received.shape
    whole = groups * stations
    scale = 1.0 / (times * width // 2)
    shape = jax.ShapeDtypeStruct((channels, whole, whole), F32)
    block = pl.BlockSpec((1, whole, whole), lambda c: (c, 0, 0))

    def body(received, real, imag):
        gram_kernel(scale, groups, times, received, real, imag)

    return pl.pallas_call(
        body,
        grid=(channels,),
        out_shape=(shape, shape),
        in_specs=[pl.BlockSpec((devices, None, stations, width), lambda c: (0, c, 0, 0))],
        out_specs=(block, block),
        compiler_params=pltpu.CompilerParams(vmem_limit_bytes=48 * 1024 * 1024),
        name="gram",
    )(received)


def local(voltages, delays, fringe, fringe_rate, filter_taps):
    samples = voltages.shape[2]
    stations = voltages.shape[1]
    frames = samples // C
    turned = front(voltages, delays, fringe, fringe_rate, filter_taps)
    groups, times = lax.axis_size("stn"), lax.axis_size("tm")
    devices = groups * times
    outgoing = turned.reshape(devices, C // devices, stations, 2 * frames)
    received = lax.all_to_all(outgoing, ("stn", "tm"), split_axis=0, concat_axis=0, tiled=True)
    return gram(received, groups, times)


def solution(mesh):
    return jax.shard_map(
        local,
        mesh=mesh,
        in_specs=(P(None, "stn", "tm"), P("stn"), P("stn"), P("stn"), P()),
        out_specs=(P(("stn", "tm"), None, None), P(("stn", "tm"), None, None)),
        check_vma=False,
    )
```

```python
import math

import jax
import jax.numpy as jnp
import numpy as np
from jax import lax
from jax.experimental import pallas as pl
from jax.experimental.pallas import tpu as pltpu
from jax.sharding import PartitionSpec as P

C = 1024
P_SIZE = 16
Q = 4096
DMAX = 2048
LANES = 128
SUB = 8
RADIX = 4
K = C // RADIX
TWO_PI = 2.0 * math.pi
BF16 = jnp.bfloat16
F32 = jnp.float32


def from_behind(block, axis, distance):
    devices = range(lax.axis_size(axis))
    route = [(i - distance, i) for i in devices if i - distance in devices]
    return lax.ppermute(block, axis, route)


def dft_table():
    k, n = np.arange(K)[:, None], np.arange(K)[None, :]
    blocks = []
    for g in range(RADIX):
        angle = ((RADIX * n - g) * k % C) * (TWO_PI / C)
        blocks.append(np.concatenate([np.cos(angle), np.sin(angle)], axis=1))
    return np.concatenate(blocks).astype(BF16)


EARLY = DMAX // LANES
LATE = (P_SIZE - 1) * C // LANES
ROW_PAD = 16
ROW_END = 9
STEP = SUB + 1


def phase_rows(fringe, fringe_rate, stations, phases):
    row = lax.broadcasted_iota(jnp.int32, (SUB, LANES), 0)
    lane = lax.broadcasted_iota(jnp.int32, (SUB, LANES), 1)
    turn = (row & 1).astype(F32) * (math.pi / 2)
    for s in range(stations):
        rest = fringe_rate[s] & (RADIX - 1)
        for half in range(K // LANES):
            sample = lane + half * LANES
            phase = (fringe[s] + (rest - RADIX * sample) * (row >> 1)) & (Q - 1)
            angle = phase.astype(F32) * (TWO_PI / Q) - turn
            top = (half * stations + s) * SUB
            phases[top : top + SUB, :] = jnp.cos(angle) * (1.0 / math.sqrt(C))


def tap_rows(filter_taps, fringe_rate, stations, pair, taps):
    for p in range(P_SIZE):
        for j in range(SUB):
            piece = filter_taps[p : p + 1, j * LANES : (j + 1) * LANES]
            for copy in range(2):
                row = SUB + (2 * p + copy) * SUB + j
                pair[row : row + 1, :] = piece
    lane = lax.broadcasted_iota(jnp.int32, (SUB, LANES), 1)

    def body(s, carry):
        delta = -(fringe_rate[s] >> 2)
        shift = delta & (LANES - 1)
        keep = lane < LANES - shift
        for p in range(P_SIZE):
            base = SUB + 2 * p * SUB - (delta >> 7)
            here = pair[pl.ds(base, SUB), :]
            before = pair[pl.ds(base - 1, SUB), :]
            top = pl.multiple_of(s * (P_SIZE * SUB), SUB) + p * SUB
            taps[pl.ds(top, SUB), :] = pltpu.roll(jnp.where(keep, here, before), shift, 1)
        return carry

    lax.fori_loop(0, stations, body, 0)


def spread(source, first, count, offset, stations, row_step, lin):
    unroll = 8

    def body(step, carry):
        for inner in range(unroll):
            block = step * unroll + inner
            lanes = pl.ds(pl.multiple_of((first + block) * LANES, LANES), LANES)
            for part in range(2):
                tile = source[part, :, lanes].astype(F32)
                for top in range(0, stations, SUB):
                    start = (part * stations + top) * row_step + ROW_PAD + offset + block
                    lin[pl.ds(start, SUB, stride=row_step), :] = tile[top : top + SUB]
        return carry

    lax.fori_loop(0, count // unroll, body, 0)


def filter_frames(delays, fringe_rate, taps, stations, frames, row_step, lin, filt):
    lane = lax.broadcasted_iota(jnp.int32, (SUB, LANES), 1)
    flat = lax.broadcasted_iota(jnp.int32, (SUB, LANES), 0) * LANES + lane

    def filter_row(row, carry):
        s = row % stations
        moved = fringe_rate[s] >> 2
        delta = delays[s] - moved
        shift = delta & (LANES - 1)
        base = row * row_step + ROW_PAD + EARLY - (delta >> 7)
        keep = lane < LANES - shift
        inner = flat < C - moved
        top = pl.multiple_of(s * (P_SIZE * SUB), SUB)

        def shifted(k):
            here = lin[pl.ds(base + SUB * k, SUB), :]
            before = lin[pl.ds(base + SUB * k - 1, SUB), :]
            return pltpu.roll(jnp.where(keep, here, before), shift, 1)

        sums = {}
        last = shifted(-1)
        for k in range(frames + P_SIZE - 1):
            now = shifted(k)
            frame = jnp.where(inner, now, last)
            last = now
            for p in range(P_SIZE):
                m = k - p
                if 0 <= m < frames:
                    term = taps[pl.ds(top + SUB * p, SUB), :] * frame
                    sums[m] = sums[m] + term if m in sums else term
            m = k - (P_SIZE - 1)
            if m >= 0:
                filt[pl.ds((row * frames + m) * STEP, SUB), :] = sums.pop(m)
        return carry

    lax.fori_loop(0, 2 * stations, filter_row, 0, unroll=2)


def butterflies(phases, stations, frames, filt, zs, top=0):
    def body(s, carry):
        def load(part, j):
            start = (part * stations + s) * (frames * STEP) + j
            return filt[pl.ds(start, frames, stride=STEP), :]

        for half in range(2):
            re = [load(0, 2 * q + half) for q in range(4)]
            im = [load(1, 2 * q + half) for q in range(4)]
            re_e, re_d = re[0] + re[2], re[0] - re[2]
            im_e, im_d = im[0] + im[2], im[0] - im[2]
            re_f, re_g = re[1] + re[3], re[1] - re[3]
            im_f, im_g = im[1] + im[3], im[1] - im[3]
            z = [
                (re_e + re_f, im_e + im_f),
                (re_d + im_g, im_d - re_g),
                (re_e - re_f, im_e - im_f),
                (re_d - im_g, im_d + re_g),
            ]
            for r in range(RADIX):
                cosine = phases[pl.ds((half * stations + s) * SUB + 2 * r, 1), :]
                sine = phases[pl.ds((half * stations + s) * SUB + 2 * r + 1, 1), :]
                zr = z[r][0] * cosine - z[r][1] * sine
                zi = z[r][0] * sine + z[r][1] * cosine
                zs[s, r, top : top + frames, pl.ds(half * LANES, LANES)] = zr.astype(BF16)
                zs[s, r, top : top + frames, pl.ds(K + half * LANES, LANES)] = zi.astype(BF16)
        return carry

    lax.fori_loop(0, stations, body, 0)


def rims_kernel(volts, early, late, sems):
    samples = volts.shape[2]
    size = early.shape[2]
    copies = [
        pltpu.make_async_copy(
            volts.at[:, :, pl.ds(0, late.shape[2])], late, sems.at[0]
        ),
        pltpu.make_async_copy(
            volts.at[:, :, pl.ds(samples - size, size)], early, sems.at[1]
        ),
    ]
    for copy in copies:
        copy.start()
    for copy in copies:
        copy.wait()


def first_kernel(
    delays, fringe, fringe_rate, volts, filter_taps, zs, phases, taps, pair, lin, filt
):
    stations = volts.shape[1]
    frames = zs.shape[2]
    row_step = lin.shape[0] // (2 * stations)
    phase_rows(fringe, fringe_rate, stations, phases)
    tap_rows(filter_taps, fringe_rate, stations, pair, taps)
    blocks = (frames + P_SIZE - 1) * SUB + EARLY
    spread(volts, P_SIZE * SUB - EARLY, blocks, 0, stations, row_step, lin)
    filter_frames(delays, fringe_rate, taps, stations, frames, row_step, lin, filt)
    butterflies(phases, stations, frames, filt, zs)


def second_kernel(
    delays, fringe_rate, volts, early, late, taps, table, phases, before, out,
    lin, filt, zs, turned
):
    stations, blocks = volts.shape[1], volts.shape[2] // LANES
    frames = zs.shape[2]
    width = 2 * (before.shape[2] + frames)
    row_step = lin.shape[0] // (2 * stations)
    spread(early, 0, EARLY, 0, stations, row_step, lin)
    spread(volts, 0, (2 * P_SIZE - 1) * SUB, EARLY, stations, row_step, lin)
    filter_frames(delays, fringe_rate, taps, stations, P_SIZE, row_step, lin, filt)
    butterflies(phases, stations, P_SIZE, filt, zs)
    own = P_SIZE * SUB + EARLY
    spread(volts, blocks - own, own, 0, stations, row_step, lin)
    spread(late, 0, LATE, own, stations, row_step, lin)
    filter_frames(delays, fringe_rate, taps, stations, P_SIZE, row_step, lin, filt)
    butterflies(phases, stations, P_SIZE, filt, zs, P_SIZE)
    step = stations + 1
    for s in range(stations):
        rest = fringe_rate[s] & (RADIX - 1)
        weights = table[pl.ds(pl.multiple_of(rest * K, K), K), :]
        sides = []
        for r in range(RADIX):
            z = jnp.concatenate([before[s, r], zs[s, r]], axis=0)
            sides += [z, jnp.concatenate([z[:, K:], -z[:, :K]], axis=1)]
        spec = lax.dot_general(
            weights,
            jnp.concatenate(sides, axis=0),
            (((1,), (1,)), ((), ())),
            preferred_element_type=F32,
        )
        for r in range(RADIX):
            part = spec[:, r * width : (r + 1) * width]
            turned[pl.ds(r * (K * step) + s, K, stride=step), :] = part
    for k in range(K):
        for r in range(RADIX):
            top = (r * K + k) * step
            out[k, r] = turned[top : top + stations, :].astype(BF16)


def rows_of(count):
    return -(-count // SUB) * SUB


def front(voltages, delays, fringe, fringe_rate, filter_taps):
    stations, samples = voltages.shape[1], voltages.shape[2]
    frames = samples // C
    rest = 2 * P_SIZE
    ahead = frames - rest
    vmem = pl.BlockSpec(memory_space=pltpu.VMEM)
    smem = pl.BlockSpec(memory_space=pltpu.SMEM)
    anywhere = pl.BlockSpec(memory_space=pl.ANY)
    estimate = pl.CostEstimate(flops=10**10, bytes_accessed=2**23, transcendentals=0)
    early, late = pl.pallas_call(
        rims_kernel,
        out_shape=[
            jax.ShapeDtypeStruct((2, stations, DMAX), BF16),
            jax.ShapeDtypeStruct((2, stations, (P_SIZE - 1) * C), BF16),
        ],
        in_specs=[anywhere],
        out_specs=[vmem, vmem],
        scratch_shapes=[pltpu.SemaphoreType.DMA((2,))],
        compiler_params=pltpu.CompilerParams(vmem_limit_bytes=57 * 2**20),
        name="rims",
    )(voltages)
    late = from_behind(late, "tm", -1)
    early = from_behind(early, "tm", 1)
    step = ROW_PAD + EARLY + (ahead + P_SIZE - 1) * SUB + ROW_END
    before, phases, taps = pl.pallas_call(
        first_kernel,
        out_shape=[
            jax.ShapeDtypeStruct((stations, RADIX, ahead, 2 * K), BF16),
            jax.ShapeDtypeStruct((K // LANES * stations * SUB, LANES), F32),
            jax.ShapeDtypeStruct((stations * P_SIZE * SUB, LANES), F32),
        ],
        in_specs=[smem, smem, smem, vmem, vmem],
        out_specs=[vmem] * 3,
        scratch_shapes=[
            pltpu.VMEM(((2 * P_SIZE + 1) * SUB, LANES), F32),
            pltpu.VMEM((rows_of(2 * stations * step), LANES), F32),
            pltpu.VMEM((2 * stations * ahead * STEP, LANES), F32),
        ],
        compiler_params=pltpu.CompilerParams(vmem_limit_bytes=28 * 2**20),
        cost_estimate=estimate,
        name="first",
    )(delays, fringe, fringe_rate, voltages, filter_taps)
    step = ROW_PAD + EARLY + (2 * P_SIZE - 1) * SUB + ROW_END
    return pl.pallas_call(
        second_kernel,
        out_shape=jax.ShapeDtypeStruct((K, RADIX, stations, 2 * frames), BF16),
        in_specs=[smem] * 2 + [vmem] * 7,
        out_specs=vmem,
        scratch_shapes=[
            pltpu.VMEM((rows_of(2 * stations * step), LANES), F32),
            pltpu.VMEM((2 * stations * P_SIZE * STEP, LANES), F32),
            pltpu.VMEM((stations, RADIX, rest, 2 * K), BF16),
            pltpu.VMEM((RADIX * K * (stations + 1), 2 * frames), F32),
        ],
        compiler_params=pltpu.CompilerParams(vmem_limit_bytes=36 * 2**20),
        cost_estimate=estimate,
        name="second",
    )(
        delays, fringe_rate, voltages, early, late, taps, jnp.asarray(dft_table()), phases, before
    )


def gram_kernel(scale, groups, times, received, real, imag):
    stations, width = received.shape[1], received.shape[2]
    half = width // 2
    tiles = received[...].reshape(groups, times, stations, width)
    direct, swapped = [], []
    for t in range(times):
        tile = tiles[:, t].reshape(groups * stations, width)
        direct.append(tile)
        swapped.append(jnp.concatenate([tile[:, half:], -tile[:, :half]], axis=1))
    rows = jnp.concatenate(direct, axis=1)
    turned_rows = jnp.concatenate(swapped, axis=1)
    contract = (((1,), (1,)), ((), ()))
    real[0] = lax.dot_general(rows, rows, contract, preferred_element_type=F32) * scale
    imag[0] = lax.dot_general(turned_rows, rows, contract, preferred_element_type=F32) * scale


def gram(received, groups, times):
    devices, channels, stations, width = received.shape
    whole = groups * stations
    scale = 1.0 / (times * width // 2)
    shape = jax.ShapeDtypeStruct((channels, whole, whole), F32)
    block = pl.BlockSpec((1, whole, whole), lambda c: (c, 0, 0))

    def body(received, real, imag):
        gram_kernel(scale, groups, times, received, real, imag)

    return pl.pallas_call(
        body,
        grid=(channels,),
        out_shape=(shape, shape),
        in_specs=[pl.BlockSpec((devices, None, stations, width), lambda c: (0, c, 0, 0))],
        out_specs=(block, block),
        compiler_params=pltpu.CompilerParams(vmem_limit_bytes=48 * 1024 * 1024),
        name="gram",
    )(received)


def local(voltages, delays, fringe, fringe_rate, filter_taps):
    samples = voltages.shape[2]
    stations = voltages.shape[1]
    frames = samples // C
    turned = front(voltages, delays, fringe, fringe_rate, filter_taps)
    groups, times = lax.axis_size("stn"), lax.axis_size("tm")
    devices = groups * times
    outgoing = turned.reshape(devices, C // devices, stations, 2 * frames)
    received = lax.all_to_all(outgoing, ("stn", "tm"), split_axis=0, concat_axis=0, tiled=True)
    return gram(received, groups, times)


def solution(mesh):
    return jax.shard_map(
        local,
        mesh=mesh,
        in_specs=(P(None, "stn", "tm"), P("stn"), P("stn"), P("stn"), P()),
        out_specs=(P(("stn", "tm"), None, None), P(("stn", "tm"), None, None)),
        check_vma=False,
    )
```

```python
import math

import jax
import jax.numpy as jnp
import numpy as np
from jax import lax
from jax.experimental import pallas as pl
from jax.experimental.pallas import tpu as pltpu
from jax.sharding import PartitionSpec as P

C = 1024
P_SIZE = 16
Q = 4096
DMAX = 2048
LANES = 128
SUB = 8
RADIX = 4
K = C // RADIX
TWO_PI = 2.0 * math.pi
BF16 = jnp.bfloat16
F32 = jnp.float32


def from_behind(block, axis, distance):
    devices = range(lax.axis_size(axis))
    route = [(i - distance, i) for i in devices if i - distance in devices]
    return lax.ppermute(block, axis, route)


def dft_table():
    k, n = np.arange(K)[:, None], np.arange(K)[None, :]
    blocks = []
    for g in range(RADIX):
        angle = ((RADIX * n - g) * k % C) * (TWO_PI / C)
        blocks.append(np.concatenate([np.cos(angle), np.sin(angle)], axis=1))
    return np.concatenate(blocks).astype(BF16)


EARLY = DMAX // LANES
LATE = (P_SIZE - 1) * C // LANES
ROW_PAD = 16
ROW_END = 9
STEP = SUB + 1


def phase_rows(fringe, fringe_rate, stations, phases):
    row = lax.broadcasted_iota(jnp.int32, (SUB, LANES), 0)
    lane = lax.broadcasted_iota(jnp.int32, (SUB, LANES), 1)
    turn = (row & 1).astype(F32) * (math.pi / 2)
    for s in range(stations):
        rest = fringe_rate[s] & (RADIX - 1)
        for half in range(K // LANES):
            sample = lane + half * LANES
            phase = (fringe[s] + (rest - RADIX * sample) * (row >> 1)) & (Q - 1)
            angle = phase.astype(F32) * (TWO_PI / Q) - turn
            top = (half * stations + s) * SUB
            phases[top : top + SUB, :] = jnp.cos(angle) * (1.0 / math.sqrt(C))


def tap_rows(filter_taps, fringe_rate, stations, pair, taps):
    for p in range(P_SIZE):
        for j in range(SUB):
            piece = filter_taps[p : p + 1, j * LANES : (j + 1) * LANES]
            for copy in range(2):
                row = SUB + (2 * p + copy) * SUB + j
                pair[row : row + 1, :] = piece
    lane = lax.broadcasted_iota(jnp.int32, (SUB, LANES), 1)

    def body(s, carry):
        delta = -(fringe_rate[s] >> 2)
        shift = delta & (LANES - 1)
        keep = lane < LANES - shift
        for p in range(P_SIZE):
            base = SUB + 2 * p * SUB - (delta >> 7)
            here = pair[pl.ds(base, SUB), :]
            before = pair[pl.ds(base - 1, SUB), :]
            top = pl.multiple_of(s * (P_SIZE * SUB), SUB) + p * SUB
            taps[pl.ds(top, SUB), :] = pltpu.roll(jnp.where(keep, here, before), shift, 1)
        return carry

    lax.fori_loop(0, stations, body, 0)


def spread(source, first, count, offset, stations, row_step, lin):
    unroll = 8

    def body(step, carry):
        for inner in range(unroll):
            block = step * unroll + inner
            lanes = pl.ds(pl.multiple_of((first + block) * LANES, LANES), LANES)
            for part in range(2):
                tile = source[part, :, lanes].astype(F32)
                for top in range(0, stations, SUB):
                    start = (part * stations + top) * row_step + ROW_PAD + offset + block
                    lin[pl.ds(start, SUB, stride=row_step), :] = tile[top : top + SUB]
        return carry

    lax.fori_loop(0, count // unroll, body, 0)


def filter_frames(delays, fringe_rate, taps, stations, frames, row_step, lin, filt):
    lane = lax.broadcasted_iota(jnp.int32, (SUB, LANES), 1)
    flat = lax.broadcasted_iota(jnp.int32, (SUB, LANES), 0) * LANES + lane

    def filter_row(row, carry):
        s = row % stations
        moved = fringe_rate[s] >> 2
        delta = delays[s] - moved
        shift = delta & (LANES - 1)
        base = row * row_step + ROW_PAD + EARLY - (delta >> 7)
        keep = lane < LANES - shift
        inner = flat < C - moved
        top = pl.multiple_of(s * (P_SIZE * SUB), SUB)

        def shifted(k):
            here = lin[pl.ds(base + SUB * k, SUB), :]
            before = lin[pl.ds(base + SUB * k - 1, SUB), :]
            return pltpu.roll(jnp.where(keep, here, before), shift, 1)

        sums = {}
        last = shifted(-1)
        for k in range(frames + P_SIZE - 1):
            now = shifted(k)
            frame = jnp.where(inner, now, last)
            last = now
            for p in range(P_SIZE):
                m = k - p
                if 0 <= m < frames:
                    term = taps[pl.ds(top + SUB * p, SUB), :] * frame
                    sums[m] = sums[m] + term if m in sums else term
            m = k - (P_SIZE - 1)
            if m >= 0:
                filt[pl.ds((row * frames + m) * STEP, SUB), :] = sums.pop(m)
        return carry

    lax.fori_loop(0, 2 * stations, filter_row, 0, unroll=8)


def butterflies(phases, stations, frames, filt, zs):
    def body(s, carry):
        def load(part, j):
            start = (part * stations + s) * (frames * STEP) + j
            return filt[pl.ds(start, frames, stride=STEP), :]

        for half in range(2):
            re = [load(0, 2 * q + half) for q in range(4)]
            im = [load(1, 2 * q + half) for q in range(4)]
            re_e, re_d = re[0] + re[2], re[0] - re[2]
            im_e, im_d = im[0] + im[2], im[0] - im[2]
            re_f, re_g = re[1] + re[3], re[1] - re[3]
            im_f, im_g = im[1] + im[3], im[1] - im[3]
            z = [
                (re_e + re_f, im_e + im_f),
                (re_d + im_g, im_d - re_g),
                (re_e - re_f, im_e - im_f),
                (re_d - im_g, im_d + re_g),
            ]
            for r in range(RADIX):
                cosine = phases[pl.ds((half * stations + s) * SUB + 2 * r, 1), :]
                sine = phases[pl.ds((half * stations + s) * SUB + 2 * r + 1, 1), :]
                zr = z[r][0] * cosine - z[r][1] * sine
                zi = z[r][0] * sine + z[r][1] * cosine
                zs[s, r, :, pl.ds(half * LANES, LANES)] = zr.astype(BF16)
                zs[s, r, :, pl.ds(K + half * LANES, LANES)] = zi.astype(BF16)
        return carry

    lax.fori_loop(0, stations, body, 0)


def rims_kernel(volts, early, late, sems):
    samples = volts.shape[2]
    size = early.shape[2]
    copies = [
        pltpu.make_async_copy(
            volts.at[:, :, pl.ds(0, late.shape[2])], late, sems.at[0]
        ),
        pltpu.make_async_copy(
            volts.at[:, :, pl.ds(samples - size, size)], early, sems.at[1]
        ),
    ]
    for copy in copies:
        copy.start()
    for copy in copies:
        copy.wait()


def first_kernel(
    delays, fringe, fringe_rate, volts, early, filter_taps, zs, phases, taps, pair, lin, filt
):
    stations = volts.shape[1]
    frames = zs.shape[2]
    row_step = lin.shape[0] // (2 * stations)
    phase_rows(fringe, fringe_rate, stations, phases)
    tap_rows(filter_taps, fringe_rate, stations, pair, taps)
    spread(early, 0, EARLY, 0, stations, row_step, lin)
    spread(volts, 0, (frames + P_SIZE - 1) * SUB, EARLY, stations, row_step, lin)
    filter_frames(delays, fringe_rate, taps, stations, frames, row_step, lin, filt)
    butterflies(phases, stations, frames, filt, zs)


def second_kernel(
    delays, fringe_rate, volts, late, taps, table, phases, before, out,
    lin, filt, zs, turned
):
    stations, blocks = volts.shape[1], volts.shape[2] // LANES
    frames = zs.shape[2]
    width = 2 * (before.shape[2] + frames)
    row_step = lin.shape[0] // (2 * stations)
    own = P_SIZE * SUB + EARLY
    spread(volts, blocks - own, own, 0, stations, row_step, lin)
    spread(late, 0, LATE, own, stations, row_step, lin)
    filter_frames(delays, fringe_rate, taps, stations, P_SIZE, row_step, lin, filt)
    butterflies(phases, stations, P_SIZE, filt, zs)
    step = stations + 1
    for s in range(stations):
        rest = fringe_rate[s] & (RADIX - 1)
        weights = table[pl.ds(pl.multiple_of(rest * K, K), K), :]
        sides = []
        for r in range(RADIX):
            z = jnp.concatenate([before[s, r], zs[s, r]], axis=0)
            sides += [z, jnp.concatenate([z[:, K:], -z[:, :K]], axis=1)]
        spec = lax.dot_general(
            weights,
            jnp.concatenate(sides, axis=0),
            (((1,), (1,)), ((), ())),
            preferred_element_type=F32,
        )
        for r in range(RADIX):
            part = spec[:, r * width : (r + 1) * width]
            turned[pl.ds(r * (K * step) + s, K, stride=step), :] = part
    for k in range(K):
        for r in range(RADIX):
            top = (r * K + k) * step
            out[k, r] = turned[top : top + stations, :].astype(BF16)


def rows_of(count):
    return -(-count // SUB) * SUB


def front(voltages, delays, fringe, fringe_rate, filter_taps):
    stations, samples = voltages.shape[1], voltages.shape[2]
    frames = samples // C
    rest = P_SIZE
    ahead = frames - rest
    vmem = pl.BlockSpec(memory_space=pltpu.VMEM)
    smem = pl.BlockSpec(memory_space=pltpu.SMEM)
    anywhere = pl.BlockSpec(memory_space=pl.ANY)
    estimate = pl.CostEstimate(flops=10**10, bytes_accessed=2**23, transcendentals=0)
    early, late = pl.pallas_call(
        rims_kernel,
        out_shape=[
            jax.ShapeDtypeStruct((2, stations, DMAX), BF16),
            jax.ShapeDtypeStruct((2, stations, (P_SIZE - 1) * C), BF16),
        ],
        in_specs=[anywhere],
        out_specs=[vmem, vmem],
        scratch_shapes=[pltpu.SemaphoreType.DMA((2,))],
        compiler_params=pltpu.CompilerParams(vmem_limit_bytes=57 * 2**20),
        name="rims",
    )(voltages)
    early = from_behind(early, "tm", 1)
    late = from_behind(late, "tm", -1)
    step = ROW_PAD + EARLY + (ahead + P_SIZE - 1) * SUB + ROW_END
    before, phases, taps = pl.pallas_call(
        first_kernel,
        out_shape=[
            jax.ShapeDtypeStruct((stations, RADIX, ahead, 2 * K), BF16),
            jax.ShapeDtypeStruct((K // LANES * stations * SUB, LANES), F32),
            jax.ShapeDtypeStruct((stations * P_SIZE * SUB, LANES), F32),
        ],
        in_specs=[smem, smem, smem, vmem, vmem, vmem],
        out_specs=[vmem] * 3,
        scratch_shapes=[
            pltpu.VMEM(((2 * P_SIZE + 1) * SUB, LANES), F32),
            pltpu.VMEM((rows_of(2 * stations * step), LANES), F32),
            pltpu.VMEM((2 * stations * ahead * STEP, LANES), F32),
        ],
        compiler_params=pltpu.CompilerParams(vmem_limit_bytes=28 * 2**20),
        cost_estimate=estimate,
        name="first",
    )(delays, fringe, fringe_rate, voltages, early, filter_taps)
    step = ROW_PAD + EARLY + (2 * P_SIZE - 1) * SUB + ROW_END
    return pl.pallas_call(
        second_kernel,
        out_shape=jax.ShapeDtypeStruct((K, RADIX, stations, 2 * frames), BF16),
        in_specs=[smem] * 2 + [vmem] * 6,
        out_specs=vmem,
        scratch_shapes=[
            pltpu.VMEM((rows_of(2 * stations * step), LANES), F32),
            pltpu.VMEM((2 * stations * P_SIZE * STEP, LANES), F32),
            pltpu.VMEM((stations, RADIX, rest, 2 * K), BF16),
            pltpu.VMEM((RADIX * K * (stations + 1), 2 * frames), F32),
        ],
        compiler_params=pltpu.CompilerParams(vmem_limit_bytes=36 * 2**20),
        cost_estimate=estimate,
        name="second",
    )(
        delays, fringe_rate, voltages, late, taps, jnp.asarray(dft_table()), phases, before
    )


def gram_kernel(scale, groups, times, received, real, imag):
    stations, width = received.shape[2], received.shape[3]
    half = width // 2
    channel = pl.program_id(0)
    tiles = received[:, channel].reshape(groups, times, stations, width)
    direct, swapped = [], []
    for t in range(times):
        tile = tiles[:, t].reshape(groups * stations, width)
        direct.append(tile)
        swapped.append(jnp.concatenate([tile[:, half:], -tile[:, :half]], axis=1))
    rows = jnp.concatenate(direct, axis=1)
    turned_rows = jnp.concatenate(swapped, axis=1)
    contract = (((1,), (1,)), ((), ()))
    real[0] = lax.dot_general(rows, rows, contract, preferred_element_type=F32) * scale
    imag[0] = lax.dot_general(turned_rows, rows, contract, preferred_element_type=F32) * scale


def gram(received, groups, times):
    devices, channels, stations, width = received.shape
    whole = groups * stations
    scale = 1.0 / (times * width // 2)
    shape = jax.ShapeDtypeStruct((channels, whole, whole), F32)
    block = pl.BlockSpec((1, whole, whole), lambda c: (c, 0, 0))

    def body(received, real, imag):
        gram_kernel(scale, groups, times, received, real, imag)

    return pl.pallas_call(
        body,
        grid=(channels,),
        out_shape=(shape, shape),
        in_specs=[pl.BlockSpec(memory_space=pltpu.VMEM)],
        out_specs=(block, block),
        compiler_params=pltpu.CompilerParams(vmem_limit_bytes=48 * 1024 * 1024),
        name="gram",
    )(received)


def local(voltages, delays, fringe, fringe_rate, filter_taps):
    samples = voltages.shape[2]
    stations = voltages.shape[1]
    frames = samples // C
    turned = front(voltages, delays, fringe, fringe_rate, filter_taps)
    groups, times = lax.axis_size("stn"), lax.axis_size("tm")
    devices = groups * times
    outgoing = turned.reshape(devices, C // devices, stations, 2 * frames)
    received = lax.all_to_all(outgoing, ("stn", "tm"), split_axis=0, concat_axis=0, tiled=True)
    return gram(received, groups, times)


def solution(mesh):
    return jax.shard_map(
        local,
        mesh=mesh,
        in_specs=(P(None, "stn", "tm"), P("stn"), P("stn"), P("stn"), P()),
        out_specs=(P(("stn", "tm"), None, None), P(("stn", "tm"), None, None)),
        check_vma=False,
    )
```

```python
import math

import jax
import jax.numpy as jnp
import numpy as np
from jax import lax
from jax.experimental import pallas as pl
from jax.experimental.pallas import tpu as pltpu
from jax.sharding import PartitionSpec as P

C = 1024
P_SIZE = 16
Q = 4096
DMAX = 2048
LANES = 128
SUB = 8
RADIX = 4
K = C // RADIX
TWO_PI = 2.0 * math.pi
BF16 = jnp.bfloat16
F32 = jnp.float32


def from_behind(block, axis, distance):
    devices = range(lax.axis_size(axis))
    route = [(i - distance, i) for i in devices if i - distance in devices]
    return lax.ppermute(block, axis, route)


def dft_table():
    k, n = np.arange(K)[:, None], np.arange(K)[None, :]
    blocks = []
    for g in range(RADIX):
        angle = ((RADIX * n - g) * k % C) * (TWO_PI / C)
        blocks.append(np.concatenate([np.cos(angle), np.sin(angle)], axis=1))
    return np.concatenate(blocks).astype(BF16)


EARLY = DMAX // LANES
LATE = (P_SIZE - 1) * C // LANES
ROW_PAD = 16
ROW_END = 9
STEP = SUB + 1


def phase_rows(fringe, fringe_rate, stations, phases):
    row = lax.broadcasted_iota(jnp.int32, (SUB, LANES), 0)
    lane = lax.broadcasted_iota(jnp.int32, (SUB, LANES), 1)
    turn = (row & 1).astype(F32) * (math.pi / 2)
    for s in range(stations):
        rest = fringe_rate[s] & (RADIX - 1)
        for half in range(K // LANES):
            sample = lane + half * LANES
            phase = (fringe[s] + (rest - RADIX * sample) * (row >> 1)) & (Q - 1)
            angle = phase.astype(F32) * (TWO_PI / Q) - turn
            top = (half * stations + s) * SUB
            phases[top : top + SUB, :] = jnp.cos(angle) * (1.0 / math.sqrt(C))


def tap_rows(filter_taps, fringe_rate, stations, pair, taps):
    for p in range(0, P_SIZE, SUB):
        for j in range(SUB):
            piece = filter_taps[p : p + SUB, j * LANES : (j + 1) * LANES]
            for copy in range(2):
                start = SUB + (2 * p + copy) * SUB + j
                pair[pl.ds(start, SUB, stride=2 * SUB), :] = piece
    lane = lax.broadcasted_iota(jnp.int32, (SUB, LANES), 1)

    def body(s, carry):
        delta = -(fringe_rate[s] >> 2)
        shift = delta & (LANES - 1)
        keep = lane < LANES - shift
        for p in range(P_SIZE):
            base = SUB + 2 * p * SUB - (delta >> 7)
            here = pair[pl.ds(base, SUB), :]
            before = pair[pl.ds(base - 1, SUB), :]
            top = pl.multiple_of(s * (P_SIZE * SUB), SUB) + p * SUB
            taps[pl.ds(top, SUB), :] = pltpu.roll(jnp.where(keep, here, before), shift, 1)
        return carry

    lax.fori_loop(0, stations, body, 0, unroll=4)


def spread(source, first, count, offset, stations, row_step, lin):
    unroll = 8

    def body(step, carry):
        for inner in range(unroll):
            block = step * unroll + inner
            lanes = pl.ds(pl.multiple_of((first + block) * LANES, LANES), LANES)
            for part in range(2):
                tile = source[part, :, lanes].astype(F32)
                for top in range(0, stations, SUB):
                    start = (part * stations + top) * row_step + ROW_PAD + offset + block
                    lin[pl.ds(start, SUB, stride=row_step), :] = tile[top : top + SUB]
        return carry

    lax.fori_loop(0, count // unroll, body, 0)


def filter_frames(delays, fringe_rate, taps, stations, frames, row_step, lin, filt):
    lane = lax.broadcasted_iota(jnp.int32, (SUB, LANES), 1)
    flat = lax.broadcasted_iota(jnp.int32, (SUB, LANES), 0) * LANES + lane

    def filter_row(row, carry):
        s = row % stations
        moved = fringe_rate[s] >> 2
        delta = delays[s] - moved
        shift = delta & (LANES - 1)
        base = row * row_step + ROW_PAD + EARLY - (delta >> 7)
        keep = lane < LANES - shift
        inner = flat < C - moved
        top = pl.multiple_of(s * (P_SIZE * SUB), SUB)

        def shifted(k):
            here = lin[pl.ds(base + SUB * k, SUB), :]
            before = lin[pl.ds(base + SUB * k - 1, SUB), :]
            return pltpu.roll(jnp.where(keep, here, before), shift, 1)

        sums = {}
        last = shifted(-1)
        for k in range(frames + P_SIZE - 1):
            now = shifted(k)
            frame = jnp.where(inner, now, last)
            last = now
            for p in range(P_SIZE):
                m = k - p
                if 0 <= m < frames:
                    term = taps[pl.ds(top + SUB * p, SUB), :] * frame
                    sums[m] = sums[m] + term if m in sums else term
            m = k - (P_SIZE - 1)
            if m >= 0:
                filt[pl.ds((row * frames + m) * STEP, SUB), :] = sums.pop(m)
        return carry

    lax.fori_loop(0, 2 * stations, filter_row, 0, unroll=8)


def butterflies(phases, stations, frames, filt, zs):
    def body(s, carry):
        def load(part, j):
            start = (part * stations + s) * (frames * STEP) + j
            return filt[pl.ds(start, frames, stride=STEP), :]

        for half in range(2):
            re = [load(0, 2 * q + half) for q in range(4)]
            im = [load(1, 2 * q + half) for q in range(4)]
            re_e, re_d = re[0] + re[2], re[0] - re[2]
            im_e, im_d = im[0] + im[2], im[0] - im[2]
            re_f, re_g = re[1] + re[3], re[1] - re[3]
            im_f, im_g = im[1] + im[3], im[1] - im[3]
            z = [
                (re_e + re_f, im_e + im_f),
                (re_d + im_g, im_d - re_g),
                (re_e - re_f, im_e - im_f),
                (re_d - im_g, im_d + re_g),
            ]
            for r in range(RADIX):
                cosine = phases[pl.ds((half * stations + s) * SUB + 2 * r, 1), :]
                sine = phases[pl.ds((half * stations + s) * SUB + 2 * r + 1, 1), :]
                zr = z[r][0] * cosine - z[r][1] * sine
                zi = z[r][0] * sine + z[r][1] * cosine
                zs[s, r, :, pl.ds(half * LANES, LANES)] = zr.astype(BF16)
                zs[s, r, :, pl.ds(K + half * LANES, LANES)] = zi.astype(BF16)
        return carry

    lax.fori_loop(0, stations, body, 0)


def rims_kernel(volts, early, late, sems):
    samples = volts.shape[2]
    size = early.shape[2]
    copies = [
        pltpu.make_async_copy(
            volts.at[:, :, pl.ds(0, late.shape[2])], late, sems.at[0]
        ),
        pltpu.make_async_copy(
            volts.at[:, :, pl.ds(samples - size, size)], early, sems.at[1]
        ),
    ]
    for copy in copies:
        copy.start()
    for copy in copies:
        copy.wait()


def first_kernel(
    delays, fringe, fringe_rate, volts, early, filter_taps, zs, phases, taps, pair, lin, filt
):
    stations = volts.shape[1]
    frames = zs.shape[2]
    row_step = lin.shape[0] // (2 * stations)
    phase_rows(fringe, fringe_rate, stations, phases)
    tap_rows(filter_taps, fringe_rate, stations, pair, taps)
    spread(early, 0, EARLY, 0, stations, row_step, lin)
    spread(volts, 0, (frames + P_SIZE - 1) * SUB, EARLY, stations, row_step, lin)
    filter_frames(delays, fringe_rate, taps, stations, frames, row_step, lin, filt)
    butterflies(phases, stations, frames, filt, zs)


def second_kernel(
    delays, fringe_rate, volts, late, taps, table, phases, before, out,
    lin, filt, zs, turned
):
    stations, blocks = volts.shape[1], volts.shape[2] // LANES
    frames = zs.shape[2]
    width = 2 * (before.shape[2] + frames)
    row_step = lin.shape[0] // (2 * stations)
    own = P_SIZE * SUB + EARLY
    spread(volts, blocks - own, own, 0, stations, row_step, lin)
    spread(late, 0, LATE, own, stations, row_step, lin)
    filter_frames(delays, fringe_rate, taps, stations, P_SIZE, row_step, lin, filt)
    butterflies(phases, stations, P_SIZE, filt, zs)
    step = stations + 1
    for s in range(stations):
        rest = fringe_rate[s] & (RADIX - 1)
        weights = table[pl.ds(pl.multiple_of(rest * K, K), K), :]
        sides = []
        for r in range(RADIX):
            z = jnp.concatenate([before[s, r], zs[s, r]], axis=0)
            sides += [z, jnp.concatenate([z[:, K:], -z[:, :K]], axis=1)]
        spec = lax.dot_general(
            weights,
            jnp.concatenate(sides, axis=0),
            (((1,), (1,)), ((), ())),
            preferred_element_type=F32,
        )
        for r in range(RADIX):
            part = spec[:, r * width : (r + 1) * width]
            turned[pl.ds(r * (K * step) + s, K, stride=step), :] = part
    for k in range(K):
        for r in range(RADIX):
            top = (r * K + k) * step
            out[k, r] = turned[top : top + stations, :].astype(BF16)


def rows_of(count):
    return -(-count // SUB) * SUB


def front(voltages, delays, fringe, fringe_rate, filter_taps):
    stations, samples = voltages.shape[1], voltages.shape[2]
    frames = samples // C
    rest = P_SIZE
    ahead = frames - rest
    vmem = pl.BlockSpec(memory_space=pltpu.VMEM)
    smem = pl.BlockSpec(memory_space=pltpu.SMEM)
    anywhere = pl.BlockSpec(memory_space=pl.ANY)
    estimate = pl.CostEstimate(flops=10**10, bytes_accessed=2**23, transcendentals=0)
    early, late = pl.pallas_call(
        rims_kernel,
        out_shape=[
            jax.ShapeDtypeStruct((2, stations, DMAX), BF16),
            jax.ShapeDtypeStruct((2, stations, (P_SIZE - 1) * C), BF16),
        ],
        in_specs=[anywhere],
        out_specs=[vmem, vmem],
        scratch_shapes=[pltpu.SemaphoreType.DMA((2,))],
        compiler_params=pltpu.CompilerParams(vmem_limit_bytes=52 * 2**20),
        name="rims",
    )(voltages)
    early = from_behind(early, "tm", 1)
    late = from_behind(late, "tm", -1)
    step = ROW_PAD + EARLY + (ahead + P_SIZE - 1) * SUB + ROW_END
    before, phases, taps = pl.pallas_call(
        first_kernel,
        out_shape=[
            jax.ShapeDtypeStruct((stations, RADIX, ahead, 2 * K), BF16),
            jax.ShapeDtypeStruct((K // LANES * stations * SUB, LANES), F32),
            jax.ShapeDtypeStruct((stations * P_SIZE * SUB, LANES), F32),
        ],
        in_specs=[smem, smem, smem, vmem, vmem, vmem],
        out_specs=[vmem] * 3,
        scratch_shapes=[
            pltpu.VMEM(((2 * P_SIZE + 1) * SUB, LANES), F32),
            pltpu.VMEM((rows_of(2 * stations * step), LANES), F32),
            pltpu.VMEM((2 * stations * ahead * STEP, LANES), F32),
        ],
        compiler_params=pltpu.CompilerParams(vmem_limit_bytes=28 * 2**20),
        cost_estimate=estimate,
        name="first",
    )(delays, fringe, fringe_rate, voltages, early, filter_taps)
    step = ROW_PAD + EARLY + (2 * P_SIZE - 1) * SUB + ROW_END
    return pl.pallas_call(
        second_kernel,
        out_shape=jax.ShapeDtypeStruct((K, RADIX, stations, 2 * frames), BF16),
        in_specs=[smem] * 2 + [vmem] * 6,
        out_specs=vmem,
        scratch_shapes=[
            pltpu.VMEM((rows_of(2 * stations * step), LANES), F32),
            pltpu.VMEM((2 * stations * P_SIZE * STEP, LANES), F32),
            pltpu.VMEM((stations, RADIX, rest, 2 * K), BF16),
            pltpu.VMEM((RADIX * K * (stations + 1), 2 * frames), F32),
        ],
        compiler_params=pltpu.CompilerParams(vmem_limit_bytes=36 * 2**20),
        cost_estimate=estimate,
        name="second",
    )(
        delays, fringe_rate, voltages, late, taps, jnp.asarray(dft_table()), phases, before
    )


def gram_kernel(scale, groups, times, received, real, imag):
    stations, width = received.shape[2], received.shape[3]
    half = width // 2
    channel = pl.program_id(0)
    tiles = received[:, channel].reshape(groups, times, stations, width)
    direct, swapped = [], []
    for t in range(times):
        tile = tiles[:, t].reshape(groups * stations, width)
        direct.append(tile)
        swapped.append(jnp.concatenate([tile[:, half:], -tile[:, :half]], axis=1))
    rows = jnp.concatenate(direct, axis=1)
    turned_rows = jnp.concatenate(swapped, axis=1)
    contract = (((1,), (1,)), ((), ()))
    real[0] = lax.dot_general(rows, rows, contract, preferred_element_type=F32) * scale
    imag[0] = lax.dot_general(turned_rows, rows, contract, preferred_element_type=F32) * scale


def gram(received, groups, times):
    devices, channels, stations, width = received.shape
    whole = groups * stations
    scale = 1.0 / (times * width // 2)
    shape = jax.ShapeDtypeStruct((channels, whole, whole), F32)
    block = pl.BlockSpec((1, whole, whole), lambda c: (c, 0, 0))

    def body(received, real, imag):
        gram_kernel(scale, groups, times, received, real, imag)

    return pl.pallas_call(
        body,
        grid=(channels,),
        out_shape=(shape, shape),
        in_specs=[pl.BlockSpec(memory_space=pltpu.VMEM)],
        out_specs=(block, block),
        compiler_params=pltpu.CompilerParams(vmem_limit_bytes=48 * 1024 * 1024),
        name="gram",
    )(received)


def local(voltages, delays, fringe, fringe_rate, filter_taps):
    samples = voltages.shape[2]
    stations = voltages.shape[1]
    frames = samples // C
    turned = front(voltages, delays, fringe, fringe_rate, filter_taps)
    groups, times = lax.axis_size("stn"), lax.axis_size("tm")
    devices = groups * times
    outgoing = turned.reshape(devices, C // devices, stations, 2 * frames)
    received = lax.all_to_all(outgoing, ("stn", "tm"), split_axis=0, concat_axis=0, tiled=True)
    return gram(received, groups, times)


def solution(mesh):
    return jax.shard_map(
        local,
        mesh=mesh,
        in_specs=(P(None, "stn", "tm"), P("stn"), P("stn"), P("stn"), P()),
        out_specs=(P(("stn", "tm"), None, None), P(("stn", "tm"), None, None)),
        check_vma=False,
    )
```

```python
import math

import jax
import jax.numpy as jnp
import numpy as np
from jax import lax
from jax.experimental import pallas as pl
from jax.experimental.pallas import tpu as pltpu
from jax.sharding import PartitionSpec as P

C = 1024
P_SIZE = 16
Q = 4096
DMAX = 2048
LANES = 128
SUB = 8
RADIX = 4
K = C // RADIX
TWO_PI = 2.0 * math.pi
BF16 = jnp.bfloat16
F32 = jnp.float32


def from_behind(block, axis, distance):
    devices = range(lax.axis_size(axis))
    route = [(i - distance, i) for i in devices if i - distance in devices]
    return lax.ppermute(block, axis, route)


def dft_table():
    k, n = np.arange(K)[:, None], np.arange(K)[None, :]
    blocks = []
    for g in range(RADIX):
        angle = ((RADIX * n - g) * k % C) * (TWO_PI / C)
        blocks.append(np.concatenate([np.cos(angle), np.sin(angle)], axis=1))
    return np.concatenate(blocks).astype(BF16)


EARLY = DMAX // LANES
LATE = (P_SIZE - 1) * C // LANES
ROW_PAD = 16
ROW_END = 9
STEP = SUB + 1


def phase_rows(fringe, fringe_rate, stations, phases):
    row = lax.broadcasted_iota(jnp.int32, (SUB, LANES), 0)
    lane = lax.broadcasted_iota(jnp.int32, (SUB, LANES), 1)
    turn = (row & 1).astype(F32) * (math.pi / 2)
    for s in range(stations):
        rest = fringe_rate[s] & (RADIX - 1)
        for half in range(K // LANES):
            sample = lane + half * LANES
            phase = (fringe[s] + (rest - RADIX * sample) * (row >> 1)) & (Q - 1)
            angle = phase.astype(F32) * (TWO_PI / Q) - turn
            top = (half * stations + s) * SUB
            phases[top : top + SUB, :] = jnp.cos(angle) * (1.0 / math.sqrt(C))


def tap_rows(filter_taps, fringe_rate, stations, pair, taps):
    for p in range(0, P_SIZE, SUB):
        for j in range(SUB):
            piece = filter_taps[p : p + SUB, j * LANES : (j + 1) * LANES]
            for copy in range(2):
                start = SUB + (2 * p + copy) * SUB + j
                pair[pl.ds(start, SUB, stride=2 * SUB), :] = piece
    lane = lax.broadcasted_iota(jnp.int32, (SUB, LANES), 1)

    def body(s, carry):
        delta = -(fringe_rate[s] >> 2)
        shift = delta & (LANES - 1)
        keep = lane < LANES - shift
        for p in range(P_SIZE):
            base = SUB + 2 * p * SUB - (delta >> 7)
            here = pair[pl.ds(base, SUB), :]
            before = pair[pl.ds(base - 1, SUB), :]
            top = pl.multiple_of(s * (P_SIZE * SUB), SUB) + p * SUB
            taps[pl.ds(top, SUB), :] = pltpu.roll(jnp.where(keep, here, before), shift, 1)
        return carry

    lax.fori_loop(0, stations, body, 0, unroll=4)


def spread(source, first, count, offset, stations, row_step, lin):
    unroll = 8

    def body(step, carry):
        for inner in range(unroll):
            block = step * unroll + inner
            lanes = pl.ds(pl.multiple_of((first + block) * LANES, LANES), LANES)
            for part in range(2):
                tile = source[part, :, lanes].astype(F32)
                for top in range(0, stations, SUB):
                    start = (part * stations + top) * row_step + ROW_PAD + offset + block
                    lin[pl.ds(start, SUB, stride=row_step), :] = tile[top : top + SUB]
        return carry

    steps = count // unroll
    lax.fori_loop(0, steps, body, 0, unroll=next(u for u in (5, 3, 2, 1) if steps % u == 0))


def filter_frames(delays, fringe_rate, taps, stations, frames, row_step, lin, filt):
    lane = lax.broadcasted_iota(jnp.int32, (SUB, LANES), 1)
    flat = lax.broadcasted_iota(jnp.int32, (SUB, LANES), 0) * LANES + lane

    def filter_row(row, carry):
        s = row % stations
        moved = fringe_rate[s] >> 2
        delta = delays[s] - moved
        shift = delta & (LANES - 1)
        base = row * row_step + ROW_PAD + EARLY - (delta >> 7)
        keep = lane < LANES - shift
        inner = flat < C - moved
        top = pl.multiple_of(s * (P_SIZE * SUB), SUB)

        def shifted(k):
            here = lin[pl.ds(base + SUB * k, SUB), :]
            before = lin[pl.ds(base + SUB * k - 1, SUB), :]
            return pltpu.roll(jnp.where(keep, here, before), shift, 1)

        sums = {}
        last = shifted(-1)
        for k in range(frames + P_SIZE - 1):
            now = shifted(k)
            frame = jnp.where(inner, now, last)
            last = now
            for p in range(P_SIZE):
                m = k - p
                if 0 <= m < frames:
                    term = taps[pl.ds(top + SUB * p, SUB), :] * frame
                    sums[m] = sums[m] + term if m in sums else term
            m = k - (P_SIZE - 1)
            if m >= 0:
                filt[pl.ds((row * frames + m) * STEP, SUB), :] = sums.pop(m)
        return carry

    lax.fori_loop(0, 2 * stations, filter_row, 0, unroll=8 if frames > P_SIZE else 16)


def butterflies(phases, stations, frames, filt, zs):
    def body(s, carry):
        def load(part, j):
            start = (part * stations + s) * (frames * STEP) + j
            return filt[pl.ds(start, frames, stride=STEP), :]

        for half in range(2):
            re = [load(0, 2 * q + half) for q in range(4)]
            im = [load(1, 2 * q + half) for q in range(4)]
            re_e, re_d = re[0] + re[2], re[0] - re[2]
            im_e, im_d = im[0] + im[2], im[0] - im[2]
            re_f, re_g = re[1] + re[3], re[1] - re[3]
            im_f, im_g = im[1] + im[3], im[1] - im[3]
            z = [
                (re_e + re_f, im_e + im_f),
                (re_d + im_g, im_d - re_g),
                (re_e - re_f, im_e - im_f),
                (re_d - im_g, im_d + re_g),
            ]
            for r in range(RADIX):
                cosine = phases[pl.ds((half * stations + s) * SUB + 2 * r, 1), :]
                sine = phases[pl.ds((half * stations + s) * SUB + 2 * r + 1, 1), :]
                zr = z[r][0] * cosine - z[r][1] * sine
                zi = z[r][0] * sine + z[r][1] * cosine
                zs[s, r, :, pl.ds(half * LANES, LANES)] = zr.astype(BF16)
                zs[s, r, :, pl.ds(K + half * LANES, LANES)] = zi.astype(BF16)
        return carry

    lax.fori_loop(0, stations, body, 0, unroll=4)


def rims_kernel(volts, early, late, sems):
    samples = volts.shape[2]
    size = early.shape[2]
    copies = [
        pltpu.make_async_copy(
            volts.at[:, :, pl.ds(0, late.shape[2])], late, sems.at[0]
        ),
        pltpu.make_async_copy(
            volts.at[:, :, pl.ds(samples - size, size)], early, sems.at[1]
        ),
    ]
    for copy in copies:
        copy.start()
    for copy in copies:
        copy.wait()


def first_kernel(
    delays, fringe, fringe_rate, volts, early, filter_taps, zs, phases, taps, pair, lin, filt
):
    stations = volts.shape[1]
    frames = zs.shape[2]
    row_step = lin.shape[0] // (2 * stations)
    phase_rows(fringe, fringe_rate, stations, phases)
    tap_rows(filter_taps, fringe_rate, stations, pair, taps)
    spread(early, 0, EARLY, 0, stations, row_step, lin)
    spread(volts, 0, (frames + P_SIZE - 1) * SUB, EARLY, stations, row_step, lin)
    filter_frames(delays, fringe_rate, taps, stations, frames, row_step, lin, filt)
    butterflies(phases, stations, frames, filt, zs)


def second_kernel(
    delays, fringe_rate, volts, late, taps, table, phases, before, out,
    lin, filt, zs, turned
):
    stations, blocks = volts.shape[1], volts.shape[2] // LANES
    frames = zs.shape[2]
    width = 2 * (before.shape[2] + frames)
    row_step = lin.shape[0] // (2 * stations)
    own = P_SIZE * SUB + EARLY
    spread(volts, blocks - own, own, 0, stations, row_step, lin)
    spread(late, 0, LATE, own, stations, row_step, lin)
    filter_frames(delays, fringe_rate, taps, stations, P_SIZE, row_step, lin, filt)
    butterflies(phases, stations, P_SIZE, filt, zs)
    step = stations + 1
    for s in range(stations):
        rest = fringe_rate[s] & (RADIX - 1)
        weights = table[pl.ds(pl.multiple_of(rest * K, K), K), :]
        sides = []
        for r in range(RADIX):
            z = jnp.concatenate([before[s, r], zs[s, r]], axis=0)
            sides += [z, jnp.concatenate([z[:, K:], -z[:, :K]], axis=1)]
        spec = lax.dot_general(
            weights,
            jnp.concatenate(sides, axis=0),
            (((1,), (1,)), ((), ())),
            preferred_element_type=F32,
        )
        for r in range(RADIX):
            part = spec[:, r * width : (r + 1) * width]
            turned[pl.ds(r * (K * step) + s, K, stride=step), :] = part
    for k in range(K):
        for r in range(RADIX):
            top = (r * K + k) * step
            out[k, r] = turned[top : top + stations, :].astype(BF16)


def rows_of(count):
    return -(-count // SUB) * SUB


def front(voltages, delays, fringe, fringe_rate, filter_taps):
    stations, samples = voltages.shape[1], voltages.shape[2]
    frames = samples // C
    rest = P_SIZE
    ahead = frames - rest
    vmem = pl.BlockSpec(memory_space=pltpu.VMEM)
    smem = pl.BlockSpec(memory_space=pltpu.SMEM)
    anywhere = pl.BlockSpec(memory_space=pl.ANY)
    estimate = pl.CostEstimate(flops=10**10, bytes_accessed=2**23, transcendentals=0)
    early, late = pl.pallas_call(
        rims_kernel,
        out_shape=[
            jax.ShapeDtypeStruct((2, stations, DMAX), BF16),
            jax.ShapeDtypeStruct((2, stations, (P_SIZE - 1) * C), BF16),
        ],
        in_specs=[anywhere],
        out_specs=[vmem, vmem],
        scratch_shapes=[pltpu.SemaphoreType.DMA((2,))],
        compiler_params=pltpu.CompilerParams(vmem_limit_bytes=52 * 2**20),
        name="rims",
    )(voltages)
    early = from_behind(early, "tm", 1)
    late = from_behind(late, "tm", -1)
    step = ROW_PAD + EARLY + (ahead + P_SIZE - 1) * SUB + ROW_END
    before, phases, taps = pl.pallas_call(
        first_kernel,
        out_shape=[
            jax.ShapeDtypeStruct((stations, RADIX, ahead, 2 * K), BF16),
            jax.ShapeDtypeStruct((K // LANES * stations * SUB, LANES), F32),
            jax.ShapeDtypeStruct((stations * P_SIZE * SUB, LANES), F32),
        ],
        in_specs=[smem, smem, smem, vmem, vmem, vmem],
        out_specs=[vmem] * 3,
        scratch_shapes=[
            pltpu.VMEM(((2 * P_SIZE + 1) * SUB, LANES), F32),
            pltpu.VMEM((rows_of(2 * stations * step), LANES), F32),
            pltpu.VMEM((2 * stations * ahead * STEP, LANES), F32),
        ],
        compiler_params=pltpu.CompilerParams(vmem_limit_bytes=28 * 2**20),
        cost_estimate=estimate,
        name="first",
    )(delays, fringe, fringe_rate, voltages, early, filter_taps)
    step = ROW_PAD + EARLY + (2 * P_SIZE - 1) * SUB + ROW_END
    return pl.pallas_call(
        second_kernel,
        out_shape=jax.ShapeDtypeStruct((K, RADIX, stations, 2 * frames), BF16),
        in_specs=[smem] * 2 + [vmem] * 6,
        out_specs=vmem,
        scratch_shapes=[
            pltpu.VMEM((rows_of(2 * stations * step), LANES), F32),
            pltpu.VMEM((2 * stations * P_SIZE * STEP, LANES), F32),
            pltpu.VMEM((stations, RADIX, rest, 2 * K), BF16),
            pltpu.VMEM((RADIX * K * (stations + 1), 2 * frames), F32),
        ],
        compiler_params=pltpu.CompilerParams(vmem_limit_bytes=36 * 2**20),
        cost_estimate=estimate,
        name="second",
    )(
        delays, fringe_rate, voltages, late, taps, jnp.asarray(dft_table()), phases, before
    )


def gram_kernel(scale, groups, times, received, real, imag):
    stations, width = received.shape[2], received.shape[3]
    half = width // 2
    channel = pl.program_id(0)
    tiles = received[:, channel].reshape(groups, times, stations, width)
    direct, swapped = [], []
    for t in range(times):
        tile = tiles[:, t].reshape(groups * stations, width)
        direct.append(tile)
        swapped.append(jnp.concatenate([tile[:, half:], -tile[:, :half]], axis=1))
    rows = jnp.concatenate(direct, axis=1)
    turned_rows = jnp.concatenate(swapped, axis=1)
    contract = (((1,), (1,)), ((), ()))
    real[0] = lax.dot_general(rows, rows, contract, preferred_element_type=F32) * scale
    imag[0] = lax.dot_general(turned_rows, rows, contract, preferred_element_type=F32) * scale


def gram(received, groups, times):
    devices, channels, stations, width = received.shape
    whole = groups * stations
    scale = 1.0 / (times * width // 2)
    shape = jax.ShapeDtypeStruct((channels, whole, whole), F32)
    block = pl.BlockSpec((1, whole, whole), lambda c: (c, 0, 0))

    def body(received, real, imag):
        gram_kernel(scale, groups, times, received, real, imag)

    return pl.pallas_call(
        body,
        grid=(channels,),
        out_shape=(shape, shape),
        in_specs=[pl.BlockSpec(memory_space=pltpu.VMEM)],
        out_specs=(block, block),
        compiler_params=pltpu.CompilerParams(vmem_limit_bytes=48 * 1024 * 1024),
        name="gram",
    )(received)


def local(voltages, delays, fringe, fringe_rate, filter_taps):
    samples = voltages.shape[2]
    stations = voltages.shape[1]
    frames = samples // C
    turned = front(voltages, delays, fringe, fringe_rate, filter_taps)
    groups, times = lax.axis_size("stn"), lax.axis_size("tm")
    devices = groups * times
    outgoing = turned.reshape(devices, C // devices, stations, 2 * frames)
    received = lax.all_to_all(outgoing, ("stn", "tm"), split_axis=0, concat_axis=0, tiled=True)
    return gram(received, groups, times)


def solution(mesh):
    return jax.shard_map(
        local,
        mesh=mesh,
        in_specs=(P(None, "stn", "tm"), P("stn"), P("stn"), P("stn"), P()),
        out_specs=(P(("stn", "tm"), None, None), P(("stn", "tm"), None, None)),
        check_vma=False,
    )
```

```python
import math

import jax
import jax.numpy as jnp
import numpy as np
from jax import lax
from jax.experimental import pallas as pl
from jax.experimental.pallas import tpu as pltpu
from jax.sharding import PartitionSpec as P

C = 1024
P_SIZE = 16
Q = 4096
DMAX = 2048
LANES = 128
SUB = 8
RADIX = 4
K = C // RADIX
TWO_PI = 2.0 * math.pi
BF16 = jnp.bfloat16
F32 = jnp.float32


def from_behind(block, axis, distance):
    devices = range(lax.axis_size(axis))
    route = [(i - distance, i) for i in devices if i - distance in devices]
    return lax.ppermute(block, axis, route)


def dft_table():
    k, n = np.arange(K)[:, None], np.arange(K)[None, :]
    blocks = []
    for g in range(RADIX):
        angle = ((RADIX * n - g) * k % C) * (TWO_PI / C)
        blocks.append(np.concatenate([np.cos(angle), np.sin(angle)], axis=1))
    return np.concatenate(blocks).astype(BF16)


EARLY = DMAX // LANES
LATE = (P_SIZE - 1) * C // LANES
ROW_PAD = 16
ROW_END = 9
STEP = SUB + 1


def phase_rows(fringe, fringe_rate, stations, phases):
    row = lax.broadcasted_iota(jnp.int32, (SUB, LANES), 0)
    lane = lax.broadcasted_iota(jnp.int32, (SUB, LANES), 1)
    turn = (row & 1).astype(F32) * (math.pi / 2)
    for s in range(stations):
        rest = fringe_rate[s] & (RADIX - 1)
        for half in range(K // LANES):
            sample = lane + half * LANES
            phase = (fringe[s] + (rest - RADIX * sample) * (row >> 1)) & (Q - 1)
            angle = phase.astype(F32) * (TWO_PI / Q) - turn
            top = (half * stations + s) * SUB
            phases[top : top + SUB, :] = jnp.cos(angle) * (1.0 / math.sqrt(C))


def tap_rows(filter_taps, fringe_rate, stations, pair, taps):
    for p in range(0, P_SIZE, SUB):
        for j in range(SUB):
            piece = filter_taps[p : p + SUB, j * LANES : (j + 1) * LANES]
            for copy in range(2):
                start = SUB + (2 * p + copy) * SUB + j
                pair[pl.ds(start, SUB, stride=2 * SUB), :] = piece
    lane = lax.broadcasted_iota(jnp.int32, (SUB, LANES), 1)

    def body(s, carry):
        delta = -(fringe_rate[s] >> 2)
        shift = delta & (LANES - 1)
        keep = lane < LANES - shift
        for p in range(P_SIZE):
            base = SUB + 2 * p * SUB - (delta >> 7)
            here = pair[pl.ds(base, SUB), :]
            before = pair[pl.ds(base - 1, SUB), :]
            top = pl.multiple_of(s * (P_SIZE * SUB), SUB) + p * SUB
            taps[pl.ds(top, SUB), :] = pltpu.roll(jnp.where(keep, here, before), shift, 1)
        return carry

    lax.fori_loop(0, stations, body, 0, unroll=4)


def spread(source, first, count, offset, stations, row_step, lin):
    unroll = 8

    def body(step, carry):
        for inner in range(unroll):
            block = step * unroll + inner
            lanes = pl.ds(pl.multiple_of((first + block) * LANES, LANES), LANES)
            for part in range(2):
                tile = source[part, :, lanes].astype(F32)
                for top in range(0, stations, SUB):
                    start = (part * stations + top) * row_step + ROW_PAD + offset + block
                    lin[pl.ds(start, SUB, stride=row_step), :] = tile[top : top + SUB]
        return carry

    steps = count // unroll
    lax.fori_loop(0, steps, body, 0, unroll=next(u for u in (5, 3, 2, 1) if steps % u == 0))


def filter_frames(delays, fringe_rate, taps, stations, frames, row_step, lin, filt):
    lane = lax.broadcasted_iota(jnp.int32, (SUB, LANES), 1)
    flat = lax.broadcasted_iota(jnp.int32, (SUB, LANES), 0) * LANES + lane

    def filter_row(row, carry):
        s = row % stations
        moved = fringe_rate[s] >> 2
        delta = delays[s] - moved
        shift = delta & (LANES - 1)
        base = row * row_step + ROW_PAD + EARLY - (delta >> 7)
        keep = lane < LANES - shift
        inner = flat < C - moved
        top = pl.multiple_of(s * (P_SIZE * SUB), SUB)

        def shifted(k):
            here = lin[pl.ds(base + SUB * k, SUB), :]
            before = lin[pl.ds(base + SUB * k - 1, SUB), :]
            return pltpu.roll(jnp.where(keep, here, before), shift, 1)

        sums = {}
        last = shifted(-1)
        for k in range(frames + P_SIZE - 1):
            now = shifted(k)
            frame = jnp.where(inner, now, last)
            last = now
            for p in range(P_SIZE):
                m = k - p
                if 0 <= m < frames:
                    term = taps[pl.ds(top + SUB * p, SUB), :] * frame
                    sums[m] = sums[m] + term if m in sums else term
            m = k - (P_SIZE - 1)
            if m >= 0:
                weighted = sums.pop(m).astype(BF16).astype(F32)
                filt[pl.ds((row * frames + m) * STEP, SUB), :] = weighted
        return carry

    lax.fori_loop(0, 2 * stations, filter_row, 0, unroll=8 if frames > P_SIZE else 16)


def butterflies(phases, stations, frames, filt, zs):
    def body(s, carry):
        def load(part, j):
            start = (part * stations + s) * (frames * STEP) + j
            return filt[pl.ds(start, frames, stride=STEP), :]

        for half in range(2):
            re = [load(0, 2 * q + half) for q in range(4)]
            im = [load(1, 2 * q + half) for q in range(4)]
            re_e, re_d = re[0] + re[2], re[0] - re[2]
            im_e, im_d = im[0] + im[2], im[0] - im[2]
            re_f, re_g = re[1] + re[3], re[1] - re[3]
            im_f, im_g = im[1] + im[3], im[1] - im[3]
            z = [
                (re_e + re_f, im_e + im_f),
                (re_d + im_g, im_d - re_g),
                (re_e - re_f, im_e - im_f),
                (re_d - im_g, im_d + re_g),
            ]
            for r in range(RADIX):
                cosine = phases[pl.ds((half * stations + s) * SUB + 2 * r, 1), :]
                sine = phases[pl.ds((half * stations + s) * SUB + 2 * r + 1, 1), :]
                zr = z[r][0] * cosine - z[r][1] * sine
                zi = z[r][0] * sine + z[r][1] * cosine
                zs[s, r, :, pl.ds(half * LANES, LANES)] = zr.astype(BF16)
                zs[s, r, :, pl.ds(K + half * LANES, LANES)] = zi.astype(BF16)
        return carry

    lax.fori_loop(0, stations, body, 0, unroll=4)


def rims_kernel(volts, early, late, sems):
    samples = volts.shape[2]
    size = early.shape[2]
    copies = [
        pltpu.make_async_copy(
            volts.at[:, :, pl.ds(0, late.shape[2])], late, sems.at[0]
        ),
        pltpu.make_async_copy(
            volts.at[:, :, pl.ds(samples - size, size)], early, sems.at[1]
        ),
    ]
    for copy in copies:
        copy.start()
    for copy in copies:
        copy.wait()


def first_kernel(
    delays, fringe, fringe_rate, volts, early, filter_taps, zs, phases, taps, pair, lin, filt
):
    stations = volts.shape[1]
    frames = zs.shape[2]
    row_step = lin.shape[0] // (2 * stations)
    phase_rows(fringe, fringe_rate, stations, phases)
    tap_rows(filter_taps, fringe_rate, stations, pair, taps)
    spread(early, 0, EARLY, 0, stations, row_step, lin)
    spread(volts, 0, (frames + P_SIZE - 1) * SUB, EARLY, stations, row_step, lin)
    filter_frames(delays, fringe_rate, taps, stations, frames, row_step, lin, filt)
    butterflies(phases, stations, frames, filt, zs)


def second_kernel(
    delays, fringe_rate, volts, late, taps, table, phases, before, out,
    lin, filt, zs, turned
):
    stations, blocks = volts.shape[1], volts.shape[2] // LANES
    frames = zs.shape[2]
    width = 2 * (before.shape[2] + frames)
    row_step = lin.shape[0] // (2 * stations)
    own = P_SIZE * SUB + EARLY
    spread(volts, blocks - own, own, 0, stations, row_step, lin)
    spread(late, 0, LATE, own, stations, row_step, lin)
    filter_frames(delays, fringe_rate, taps, stations, P_SIZE, row_step, lin, filt)
    butterflies(phases, stations, P_SIZE, filt, zs)
    step = stations + 1
    for s in range(stations):
        rest = fringe_rate[s] & (RADIX - 1)
        weights = table[pl.ds(pl.multiple_of(rest * K, K), K), :]
        sides = []
        for r in range(RADIX):
            z = jnp.concatenate([before[s, r], zs[s, r]], axis=0)
            sides += [z, jnp.concatenate([z[:, K:], -z[:, :K]], axis=1)]
        spec = lax.dot_general(
            weights,
            jnp.concatenate(sides, axis=0),
            (((1,), (1,)), ((), ())),
            preferred_element_type=F32,
        )
        for r in range(RADIX):
            part = spec[:, r * width : (r + 1) * width]
            turned[pl.ds(r * (K * step) + s, K, stride=step), :] = part
    for k in range(K):
        for r in range(RADIX):
            top = (r * K + k) * step
            out[k, r] = turned[top : top + stations, :].astype(BF16)


def rows_of(count):
    return -(-count // SUB) * SUB


def front(voltages, delays, fringe, fringe_rate, filter_taps):
    stations, samples = voltages.shape[1], voltages.shape[2]
    frames = samples // C
    rest = P_SIZE
    ahead = frames - rest
    vmem = pl.BlockSpec(memory_space=pltpu.VMEM)
    smem = pl.BlockSpec(memory_space=pltpu.SMEM)
    anywhere = pl.BlockSpec(memory_space=pl.ANY)
    estimate = pl.CostEstimate(flops=10**10, bytes_accessed=2**23, transcendentals=0)
    early, late = pl.pallas_call(
        rims_kernel,
        out_shape=[
            jax.ShapeDtypeStruct((2, stations, DMAX), BF16),
            jax.ShapeDtypeStruct((2, stations, (P_SIZE - 1) * C), BF16),
        ],
        in_specs=[anywhere],
        out_specs=[vmem, vmem],
        scratch_shapes=[pltpu.SemaphoreType.DMA((2,))],
        compiler_params=pltpu.CompilerParams(vmem_limit_bytes=52 * 2**20),
        name="rims",
    )(voltages)
    early = from_behind(early, "tm", 1)
    late = from_behind(late, "tm", -1)
    step = ROW_PAD + EARLY + (ahead + P_SIZE - 1) * SUB + ROW_END
    before, phases, taps = pl.pallas_call(
        first_kernel,
        out_shape=[
            jax.ShapeDtypeStruct((stations, RADIX, ahead, 2 * K), BF16),
            jax.ShapeDtypeStruct((K // LANES * stations * SUB, LANES), F32),
            jax.ShapeDtypeStruct((stations * P_SIZE * SUB, LANES), F32),
        ],
        in_specs=[smem, smem, smem, vmem, vmem, vmem],
        out_specs=[vmem] * 3,
        scratch_shapes=[
            pltpu.VMEM(((2 * P_SIZE + 1) * SUB, LANES), F32),
            pltpu.VMEM((rows_of(2 * stations * step), LANES), F32),
            pltpu.VMEM((2 * stations * ahead * STEP, LANES), F32),
        ],
        compiler_params=pltpu.CompilerParams(vmem_limit_bytes=28 * 2**20),
        cost_estimate=estimate,
        name="first",
    )(delays, fringe, fringe_rate, voltages, early, filter_taps)
    step = ROW_PAD + EARLY + (2 * P_SIZE - 1) * SUB + ROW_END
    return pl.pallas_call(
        second_kernel,
        out_shape=jax.ShapeDtypeStruct((K, RADIX, stations, 2 * frames), BF16),
        in_specs=[smem] * 2 + [vmem] * 6,
        out_specs=vmem,
        scratch_shapes=[
            pltpu.VMEM((rows_of(2 * stations * step), LANES), F32),
            pltpu.VMEM((2 * stations * P_SIZE * STEP, LANES), F32),
            pltpu.VMEM((stations, RADIX, rest, 2 * K), BF16),
            pltpu.VMEM((RADIX * K * (stations + 1), 2 * frames), F32),
        ],
        compiler_params=pltpu.CompilerParams(vmem_limit_bytes=36 * 2**20),
        cost_estimate=estimate,
        name="second",
    )(
        delays, fringe_rate, voltages, late, taps, jnp.asarray(dft_table()), phases, before
    )


def gram_kernel(scale, groups, times, received, real, imag):
    stations, width = received.shape[2], received.shape[3]
    half = width // 2
    channel = pl.program_id(0)
    tiles = received[:, channel].reshape(groups, times, stations, width)
    direct, swapped = [], []
    for t in range(times):
        tile = tiles[:, t].reshape(groups * stations, width)
        direct.append(tile)
        swapped.append(jnp.concatenate([tile[:, half:], -tile[:, :half]], axis=1))
    rows = jnp.concatenate(direct, axis=1)
    turned_rows = jnp.concatenate(swapped, axis=1)
    contract = (((1,), (1,)), ((), ()))
    real[0] = lax.dot_general(rows, rows, contract, preferred_element_type=F32) * scale
    imag[0] = lax.dot_general(turned_rows, rows, contract, preferred_element_type=F32) * scale


def gram(received, groups, times):
    devices, channels, stations, width = received.shape
    whole = groups * stations
    scale = 1.0 / (times * width // 2)
    shape = jax.ShapeDtypeStruct((channels, whole, whole), F32)
    block = pl.BlockSpec((1, whole, whole), lambda c: (c, 0, 0))

    def body(received, real, imag):
        gram_kernel(scale, groups, times, received, real, imag)

    return pl.pallas_call(
        body,
        grid=(channels,),
        out_shape=(shape, shape),
        in_specs=[pl.BlockSpec(memory_space=pltpu.VMEM)],
        out_specs=(block, block),
        compiler_params=pltpu.CompilerParams(vmem_limit_bytes=48 * 1024 * 1024),
        name="gram",
    )(received)


def local(voltages, delays, fringe, fringe_rate, filter_taps):
    samples = voltages.shape[2]
    stations = voltages.shape[1]
    frames = samples // C
    turned = front(voltages, delays, fringe, fringe_rate, filter_taps)
    groups, times = lax.axis_size("stn"), lax.axis_size("tm")
    devices = groups * times
    outgoing = turned.reshape(devices, C // devices, stations, 2 * frames)
    received = lax.all_to_all(outgoing, ("stn", "tm"), split_axis=0, concat_axis=0, tiled=True)
    return gram(received, groups, times)


def solution(mesh):
    return jax.shard_map(
        local,
        mesh=mesh,
        in_specs=(P(None, "stn", "tm"), P("stn"), P("stn"), P("stn"), P()),
        out_specs=(P(("stn", "tm"), None, None), P(("stn", "tm"), None, None)),
        check_vma=False,
    )
```

```python
import math

import jax
import jax.numpy as jnp
import numpy as np
from jax import lax
from jax.experimental import pallas as pl
from jax.experimental.pallas import tpu as pltpu
from jax.sharding import PartitionSpec as P

C = 1024
P_SIZE = 16
Q = 4096
DMAX = 2048
LANES = 128
SUB = 8
RADIX = 4
K = C // RADIX
TWO_PI = 2.0 * math.pi
BF16 = jnp.bfloat16
F32 = jnp.float32


def from_behind(block, axis, distance):
    devices = range(lax.axis_size(axis))
    route = [(i - distance, i) for i in devices if i - distance in devices]
    return lax.ppermute(block, axis, route)


def dft_table():
    k, n = np.arange(K)[:, None], np.arange(K)[None, :]
    blocks = []
    for g in range(RADIX):
        angle = ((RADIX * n - g) * k % C) * (TWO_PI / C)
        blocks.append(np.concatenate([np.cos(angle), np.sin(angle)], axis=1))
    return np.concatenate(blocks).astype(BF16)


EARLY = DMAX // LANES
LATE = (P_SIZE - 1) * C // LANES
ROW_PAD = 16
ROW_END = 9
STEP = SUB + 1


def phase_rows(fringe, fringe_rate, stations, phases):
    row = lax.broadcasted_iota(jnp.int32, (SUB, LANES), 0)
    lane = lax.broadcasted_iota(jnp.int32, (SUB, LANES), 1)
    turn = (row & 1).astype(F32) * (math.pi / 2)
    for s in range(stations):
        rest = fringe_rate[s] & (RADIX - 1)
        for half in range(K // LANES):
            sample = lane + half * LANES
            phase = (fringe[s] + (rest - RADIX * sample) * (row >> 1)) & (Q - 1)
            angle = phase.astype(F32) * (TWO_PI / Q) - turn
            top = (half * stations + s) * SUB
            phases[top : top + SUB, :] = jnp.cos(angle) * (1.0 / math.sqrt(C))


def tap_rows(filter_taps, fringe_rate, stations, pair, taps):
    for p in range(0, P_SIZE, SUB):
        for j in range(SUB):
            piece = filter_taps[p : p + SUB, j * LANES : (j + 1) * LANES]
            for copy in range(2):
                start = SUB + (2 * p + copy) * SUB + j
                pair[pl.ds(start, SUB, stride=2 * SUB), :] = piece
    lane = lax.broadcasted_iota(jnp.int32, (SUB, LANES), 1)

    def body(s, carry):
        delta = -(fringe_rate[s] >> 2)
        shift = delta & (LANES - 1)
        keep = lane < LANES - shift
        for p in range(P_SIZE):
            base = SUB + 2 * p * SUB - (delta >> 7)
            here = pair[pl.ds(base, SUB), :]
            before = pair[pl.ds(base - 1, SUB), :]
            top = pl.multiple_of(s * (P_SIZE * SUB), SUB) + p * SUB
            taps[pl.ds(top, SUB), :] = pltpu.roll(jnp.where(keep, here, before), shift, 1)
        return carry

    lax.fori_loop(0, stations, body, 0, unroll=4)


def spread(source, first, count, offset, stations, row_step, lin):
    unroll = 8

    def body(step, carry):
        for inner in range(unroll):
            block = step * unroll + inner
            lanes = pl.ds(pl.multiple_of((first + block) * LANES, LANES), LANES)
            for part in range(2):
                tile = source[part, :, lanes].astype(F32)
                for top in range(0, stations, SUB):
                    start = (part * stations + top) * row_step + ROW_PAD + offset + block
                    lin[pl.ds(start, SUB, stride=row_step), :] = tile[top : top + SUB]
        return carry

    steps = count // unroll
    lax.fori_loop(0, steps, body, 0, unroll=next(u for u in (5, 3, 2, 1) if steps % u == 0))


def filter_frames(delays, fringe_rate, taps, stations, frames, row_step, lin, filt):
    lane = lax.broadcasted_iota(jnp.int32, (SUB, LANES), 1)
    flat = lax.broadcasted_iota(jnp.int32, (SUB, LANES), 0) * LANES + lane

    def filter_row(row, carry):
        s = row % stations
        moved = fringe_rate[s] >> 2
        delta = delays[s] - moved
        shift = delta & (LANES - 1)
        base = row * row_step + ROW_PAD + EARLY - (delta >> 7)
        keep = lane < LANES - shift
        inner = flat < C - moved
        top = pl.multiple_of(s * (P_SIZE * SUB), SUB)

        def shifted(k):
            here = lin[pl.ds(base + SUB * k, SUB), :]
            before = lin[pl.ds(base + SUB * k - 1, SUB), :]
            return pltpu.roll(jnp.where(keep, here, before), shift, 1)

        sums = {}
        last = shifted(-1)
        for k in range(frames + P_SIZE - 1):
            now = shifted(k)
            frame = jnp.where(inner, now, last)
            last = now
            for p in range(P_SIZE):
                m = k - p
                if 0 <= m < frames:
                    term = taps[pl.ds(top + SUB * p, SUB), :] * frame
                    sums[m] = sums[m] + term if m in sums else term
            m = k - (P_SIZE - 1)
            if m >= 0:
                filt[pl.ds((row * frames + m) * STEP, SUB), :] = sums.pop(m)
        return carry

    lax.fori_loop(0, 2 * stations, filter_row, 0, unroll=16)


def butterflies(phases, stations, frames, filt, zs):
    def body(s, carry):
        def load(part, j):
            start = (part * stations + s) * (frames * STEP) + j
            return filt[pl.ds(start, frames, stride=STEP), :]

        for half in range(2):
            re = [load(0, 2 * q + half) for q in range(4)]
            im = [load(1, 2 * q + half) for q in range(4)]
            re_e, re_d = re[0] + re[2], re[0] - re[2]
            im_e, im_d = im[0] + im[2], im[0] - im[2]
            re_f, re_g = re[1] + re[3], re[1] - re[3]
            im_f, im_g = im[1] + im[3], im[1] - im[3]
            z = [
                (re_e + re_f, im_e + im_f),
                (re_d + im_g, im_d - re_g),
                (re_e - re_f, im_e - im_f),
                (re_d - im_g, im_d + re_g),
            ]
            for r in range(RADIX):
                cosine = phases[pl.ds((half * stations + s) * SUB + 2 * r, 1), :]
                sine = phases[pl.ds((half * stations + s) * SUB + 2 * r + 1, 1), :]
                zr = z[r][0] * cosine - z[r][1] * sine
                zi = z[r][0] * sine + z[r][1] * cosine
                zs[s, r, :, pl.ds(half * LANES, LANES)] = zr.astype(BF16)
                zs[s, r, :, pl.ds(K + half * LANES, LANES)] = zi.astype(BF16)
        return carry

    lax.fori_loop(0, stations, body, 0, unroll=4)


def rims_kernel(volts, early, late, sems):
    samples = volts.shape[2]
    size = early.shape[2]
    copies = [
        pltpu.make_async_copy(
            volts.at[:, :, pl.ds(0, late.shape[2])], late, sems.at[0]
        ),
        pltpu.make_async_copy(
            volts.at[:, :, pl.ds(samples - size, size)], early, sems.at[1]
        ),
    ]
    for copy in copies:
        copy.start()
    for copy in copies:
        copy.wait()


def first_kernel(
    delays, fringe, fringe_rate, volts, early, filter_taps, zs, phases, taps, pair, lin, filt
):
    stations = volts.shape[1]
    frames = zs.shape[2]
    row_step = lin.shape[0] // (2 * stations)
    phase_rows(fringe, fringe_rate, stations, phases)
    tap_rows(filter_taps, fringe_rate, stations, pair, taps)
    spread(early, 0, EARLY, 0, stations, row_step, lin)
    spread(volts, 0, (frames + P_SIZE - 1) * SUB, EARLY, stations, row_step, lin)
    filter_frames(delays, fringe_rate, taps, stations, frames, row_step, lin, filt)
    butterflies(phases, stations, frames, filt, zs)


def second_kernel(
    delays, fringe_rate, volts, late, taps, table, phases, before, out,
    lin, filt, zs, turned
):
    stations, blocks = volts.shape[1], volts.shape[2] // LANES
    frames = zs.shape[2]
    width = 2 * (before.shape[2] + frames)
    row_step = lin.shape[0] // (2 * stations)
    own = P_SIZE * SUB + EARLY
    spread(volts, blocks - own, own, 0, stations, row_step, lin)
    spread(late, 0, LATE, own, stations, row_step, lin)
    filter_frames(delays, fringe_rate, taps, stations, P_SIZE, row_step, lin, filt)
    butterflies(phases, stations, P_SIZE, filt, zs)
    step = stations + 1
    for s in range(stations):
        rest = fringe_rate[s] & (RADIX - 1)
        weights = table[pl.ds(pl.multiple_of(rest * K, K), K), :]
        sides = []
        for r in range(RADIX):
            z = jnp.concatenate([before[s, r], zs[s, r]], axis=0)
            sides += [z, jnp.concatenate([z[:, K:], -z[:, :K]], axis=1)]
        spec = lax.dot_general(
            weights,
            jnp.concatenate(sides, axis=0),
            (((1,), (1,)), ((), ())),
            preferred_element_type=F32,
        )
        for r in range(RADIX):
            part = spec[:, r * width : (r + 1) * width]
            turned[pl.ds(r * (K * step) + s, K, stride=step), :] = part
    for k in range(K):
        for r in range(RADIX):
            top = (r * K + k) * step
            out[k, r] = turned[top : top + stations, :].astype(BF16)


def rows_of(count):
    return -(-count // SUB) * SUB


def front(voltages, delays, fringe, fringe_rate, filter_taps):
    stations, samples = voltages.shape[1], voltages.shape[2]
    frames = samples // C
    rest = P_SIZE
    ahead = frames - rest
    vmem = pl.BlockSpec(memory_space=pltpu.VMEM)
    smem = pl.BlockSpec(memory_space=pltpu.SMEM)
    anywhere = pl.BlockSpec(memory_space=pl.ANY)
    estimate = pl.CostEstimate(flops=10**10, bytes_accessed=2**23, transcendentals=0)
    early, late = pl.pallas_call(
        rims_kernel,
        out_shape=[
            jax.ShapeDtypeStruct((2, stations, DMAX), BF16),
            jax.ShapeDtypeStruct((2, stations, (P_SIZE - 1) * C), BF16),
        ],
        in_specs=[anywhere],
        out_specs=[vmem, vmem],
        scratch_shapes=[pltpu.SemaphoreType.DMA((2,))],
        compiler_params=pltpu.CompilerParams(vmem_limit_bytes=52 * 2**20),
        name="rims",
    )(voltages)
    early = from_behind(early, "tm", 1)
    late = from_behind(late, "tm", -1)
    step = ROW_PAD + EARLY + (ahead + P_SIZE - 1) * SUB + ROW_END
    before, phases, taps = pl.pallas_call(
        first_kernel,
        out_shape=[
            jax.ShapeDtypeStruct((stations, RADIX, ahead, 2 * K), BF16),
            jax.ShapeDtypeStruct((K // LANES * stations * SUB, LANES), F32),
            jax.ShapeDtypeStruct((stations * P_SIZE * SUB, LANES), F32),
        ],
        in_specs=[smem, smem, smem, vmem, vmem, vmem],
        out_specs=[vmem] * 3,
        scratch_shapes=[
            pltpu.VMEM(((2 * P_SIZE + 1) * SUB, LANES), F32),
            pltpu.VMEM((rows_of(2 * stations * step), LANES), F32),
            pltpu.VMEM((2 * stations * ahead * STEP, LANES), F32),
        ],
        compiler_params=pltpu.CompilerParams(vmem_limit_bytes=28 * 2**20),
        cost_estimate=estimate,
        name="first",
    )(delays, fringe, fringe_rate, voltages, early, filter_taps)
    step = ROW_PAD + EARLY + (2 * P_SIZE - 1) * SUB + ROW_END
    return pl.pallas_call(
        second_kernel,
        out_shape=jax.ShapeDtypeStruct((K, RADIX, stations, 2 * frames), BF16),
        in_specs=[smem] * 2 + [vmem] * 6,
        out_specs=vmem,
        scratch_shapes=[
            pltpu.VMEM((rows_of(2 * stations * step), LANES), F32),
            pltpu.VMEM((2 * stations * P_SIZE * STEP, LANES), F32),
            pltpu.VMEM((stations, RADIX, rest, 2 * K), BF16),
            pltpu.VMEM((RADIX * K * (stations + 1), 2 * frames), F32),
        ],
        compiler_params=pltpu.CompilerParams(vmem_limit_bytes=36 * 2**20),
        cost_estimate=estimate,
        name="second",
    )(
        delays, fringe_rate, voltages, late, taps, jnp.asarray(dft_table()), phases, before
    )


def gram_kernel(scale, groups, times, received, real, imag):
    stations, width = received.shape[2], received.shape[3]
    half = width // 2
    channel = pl.program_id(0)
    tiles = received[:, channel].reshape(groups, times, stations, width)
    direct, swapped = [], []
    for t in range(times):
        tile = tiles[:, t].reshape(groups * stations, width)
        direct.append(tile)
        swapped.append(jnp.concatenate([tile[:, half:], -tile[:, :half]], axis=1))
    rows = jnp.concatenate(direct, axis=1)
    turned_rows = jnp.concatenate(swapped, axis=1)
    contract = (((1,), (1,)), ((), ()))
    real[0] = lax.dot_general(rows, rows, contract, preferred_element_type=F32) * scale
    imag[0] = lax.dot_general(turned_rows, rows, contract, preferred_element_type=F32) * scale


def gram(received, groups, times):
    devices, channels, stations, width = received.shape
    whole = groups * stations
    scale = 1.0 / (times * width // 2)
    shape = jax.ShapeDtypeStruct((channels, whole, whole), F32)
    block = pl.BlockSpec((1, whole, whole), lambda c: (c, 0, 0))

    def body(received, real, imag):
        gram_kernel(scale, groups, times, received, real, imag)

    return pl.pallas_call(
        body,
        grid=(channels,),
        out_shape=(shape, shape),
        in_specs=[pl.BlockSpec(memory_space=pltpu.VMEM)],
        out_specs=(block, block),
        compiler_params=pltpu.CompilerParams(vmem_limit_bytes=48 * 1024 * 1024),
        name="gram",
    )(received)


def local(voltages, delays, fringe, fringe_rate, filter_taps):
    samples = voltages.shape[2]
    stations = voltages.shape[1]
    frames = samples // C
    turned = front(voltages, delays, fringe, fringe_rate, filter_taps)
    groups, times = lax.axis_size("stn"), lax.axis_size("tm")
    devices = groups * times
    outgoing = turned.reshape(devices, C // devices, stations, 2 * frames)
    received = lax.all_to_all(outgoing, ("stn", "tm"), split_axis=0, concat_axis=0, tiled=True)
    return gram(received, groups, times)


def solution(mesh):
    return jax.shard_map(
        local,
        mesh=mesh,
        in_specs=(P(None, "stn", "tm"), P("stn"), P("stn"), P("stn"), P()),
        out_specs=(P(("stn", "tm"), None, None), P(("stn", "tm"), None, None)),
        check_vma=False,
    )
```
